32 devices in a mesh: grp: 8 (over z, x), exp: 4 (over y, core).
Axes of the slice: x: 2, y: 2, z: 4, core: 2. Of those that a mesh axis runs over, the one named last changes fastest.
Arguments:
- step_inputs: bfloat16 [8, 4, 4, 2048], P('grp'), may hold values from -10 to 10
- parents: int32 [8, 4, 4], P('grp'), may hold values from 0 to 7
- routes: int32 [8, 4, 4, 6], P('grp'), may hold values from 0 to 63, all different within a row; in each aligned block of 16 rows (0 to 15, 16 to 31, ..., all dimensions but the last counted through in order) at most 3 rows name the same one
- w_qkv: bfloat16 [2048, 3, 2048], P(None, None, 'exp'), may hold values from -0.125 to 0.125
- w_out: bfloat16 [2048, 2048], P('exp'), may hold values from -0.125 to 0.125
- prompt_keys: bfloat16 [8, 1024, 2048], P('grp', None, 'exp'), may hold values from -128 to 128, as said below
- prompt_values: bfloat16 [8, 1024, 2048], P('grp', None, 'exp'), may hold values from -6 to 6
- prompt_parts: int32 [8], P('grp'), may hold values from 1 to 1024, as said below
- tail_keys: bfloat16 [8, 4, 60, 2048], P('grp', None, None, 'exp'), may hold values from -18 to 18
- tail_values: bfloat16 [8, 4, 60, 2048], P('grp', None, None, 'exp'), may hold values from -6 to 6
- w_router: bfloat16 [2048, 64], P('exp'), may hold values from -0.022097087 to 0.022097087
- norm_gain: float32 [2048], P('exp'), may hold values from 0.1 to 1.9
- w_gate_up: bfloat16 [64, 2048, 2816], P('grp', 'exp'), may hold values from -0.125 to 0.125
- w_down: bfloat16 [64, 2048, 1408], P('grp', 'exp'), may hold values from -0.15625 to 0.15625
Outputs:
- layer_out: bfloat16 [8, 4, 4, 2048], P('grp', None, None, 'exp')
The draws below stay inside these ranges and needn't reach their ends.
Inputs may be any that keep to these rules, and one draw needn't show every extreme that they name: `prompt_keys`: keys of order a few units. `prompt_parts`: each part holds 1 to 1024 valid positions; in every draw some part holds exactly 1024. `routes`: within the rows of one slot no expert is named more than 3 times, and in every draw some expert is named exactly 3 times by the rows of some slot.
All inputs are finite; a program needn't handle non-finite values.
Results may differ from the reference program's by a relative error of at most 0.013.
Values may be sent and summed in bfloat16 or wider, within the bound.
No kernel may reach another device: no remote copies, remote signals or barrier semaphores. Data moves between devices by JAX's collectives and lax.ppermute only.
A program may use at most 128 MiB of HBM per device.

```python
import math
from functools import partial
import jax
import jax.numpy as jnp
import numpy as np
from jax import lax

D = 2048
HEADS = 16
HDIM = 128
EXPERTS = 64
FFE = 1408
TOPK = 6
BEAMS = 8
STEPS = 4
TAIL = 64
CAP = 1024
CAP_E = 3
SLOTS = 8
HALF = 4
PREV = 60


def draw_step_inputs(key, part):
    shape = (SLOTS, STEPS, HALF, D)
    ramp = jnp.arange(D, dtype=jnp.float32) / (D - 1.0)
    profile = jnp.exp(jnp.log(0.5) + ramp * (jnp.log(1.5) - jnp.log(0.5)))
    values = jnp.clip(jax.random.normal(key, shape, jnp.float32), -6.0, 6.0) * profile
    return values.astype(jnp.bfloat16)


def draw_prompt_keys(key, part):
    shape = (SLOTS, CAP, HEADS * HDIM)
    values = jnp.clip(jax.random.normal(key, shape, jnp.float32), -6.0, 6.0) * 3.0
    return values.astype(jnp.bfloat16)


def draw_prompt_parts(key, part):
    counts = jax.random.randint(key, (SLOTS,), 1, CAP + 1)
    filled = jax.random.randint(jax.random.fold_in(key, 3), (), 0, SLOTS)
    return jnp.where(jnp.arange(SLOTS) == filled, CAP, counts).astype(jnp.int32)


def draw_w_router(key, part):
    shape = (D, EXPERTS)
    factor = 1.0 / D ** 0.5
    values = jnp.clip(jax.random.normal(key, shape, jnp.float32) * 0.4, -1.0, 1.0) * factor
    return values.astype(jnp.bfloat16)


def with_ends(values, own_key, smallest, top_value):
    shape = values.shape
    index_at = [jax.random.randint(jax.random.fold_in(own_key, axis), (), 0, shape[axis]) for axis in range(len(shape))]
    values = values.at[tuple(index_at)].set(smallest)
    longest = shape.index(max(shape))
    index_at[longest] = (index_at[longest] + 1) % shape[longest]
    return values.at[tuple(index_at)].set(top_value)


def block_levels(own_key, dims, shards, least, high):
    def one(dim, shards_of):
        steps = jax.random.uniform(jax.random.fold_in(jax.random.fold_in(own_key, 6), dim), (shards_of,), jnp.float32, least / len(shards), high / len(shards))
        return jnp.repeat(jnp.exp(steps), dims[dim] // shards_of).reshape((-1,) + (1,) * (len(dims) - dim - 1))

    gain = one(*shards[0])
    for cut in shards[1:]:
        gain = gain * one(*cut)
    return gain


def routed_block(rng, own, number, rows, amount, top, reach, skew):
    order = jax.random.permutation(rng, amount)
    crowded, usual = portions_of(amount, rows * top, reach, skew, True), portions_of(amount, rows * top, reach, skew, False)
    places = jnp.arange(amount)

    def named(tallies, turn):
        used = int((tallies > 0).sum())
        fixed = max(1, used // 4)
        shifted = fixed + (places - fixed + turn * (used - fixed)) % max(1, amount - fixed)
        return jnp.zeros((amount,), jnp.int32).at[order[jnp.where(places < fixed, places, shifted)]].set(jnp.asarray(tallies, jnp.int32))

    tallies = jnp.where(number % 4 == 0, named(crowded, number // 4), named(usual, number - number // 4 - 1))
    mixed = jax.random.permutation(jax.random.fold_in(own, 3), amount)
    giver, taker = mixed[0:amount // 2 * 2:2], mixed[1:amount // 2 * 2:2]
    slack = jnp.minimum(tallies[giver] - 1, reach - tallies[taker]) // 2
    slack = jnp.where((giver == order[0]) | (taker == order[0]) | (tallies[taker] == 0), 0, jnp.maximum(slack, 0))
    shifted = jax.random.randint(jax.random.fold_in(own, 4), (amount // 2,), 0, 1 << 20) % (slack + 1)
    tallies = tallies.at[giver].add(-shifted).at[taker].add(shifted)
    members = jnp.searchsorted(jnp.cumsum(tallies), jnp.arange(rows * top), side="right").astype(jnp.int32)
    listing = members.reshape(top, rows).T
    listing = listing[jax.random.permutation(jax.random.fold_in(own, 1), rows)]
    turn = jax.random.randint(jax.random.fold_in(own, 2), (rows, 1), 0, top)
    return jnp.take_along_axis(listing, (jnp.arange(top)[None, :] + turn) % top, axis=1)


def portions_of(number_of, total, limit, skew, full):
    loads = [(1 << 20) // math.isqrt(grade ** skew) + 1 for grade in range(1, number_of + 1)]
    largest = limit if full else min(limit, max(-(-total // number_of), total * loads[0] // sum(loads)))
    least = 1 if total - largest >= number_of - 1 else 0
    given, surplus = [largest] + [least] * (number_of - 1), total - largest - least * (number_of - 1)
    while surplus > 0:
        candidates = [i for i in range(1, number_of) if given[i] < largest] or [i for i in range(1, number_of) if given[i] < limit]
        whole, remaining = sum([loads[i] for i in candidates]), surplus
        for i in candidates:
            more = min(limit - given[i], max(1, remaining * loads[i] // whole), surplus)
            given[i] = given[i] + more
            surplus = surplus - more
    return np.array(given)


def scatter_about(key, extent, scale, reach, cuts=(), kind=jnp.bfloat16):
    loudness = block_levels(key, extent, cuts, -0.22, 0.18) if cuts else 1.0
    values = jax.random.normal(key, extent, jnp.float32) * scale * loudness
    return jnp.minimum(jnp.maximum(values, -reach), reach).astype(kind)


def setup_inputs(seed: int = 0) -> dict:
    streams_of = jax.random.split(jax.random.key(seed), 15)
    step_inputs = draw_step_inputs(jax.random.fold_in(streams_of[14], 71), 0)
    parents = with_ends(jax.random.randint(streams_of[1], (SLOTS, STEPS, HALF), 0, BEAMS), jax.random.fold_in(streams_of[1], 1), 0, BEAMS - 1).astype(jnp.int32)
    routes_keys = jax.random.split(jax.random.fold_in(streams_of[2], 1), SLOTS * STEPS * HALF // (STEPS * HALF))
    routes_turns = jax.random.permutation(jax.random.fold_in(streams_of[2], 3), SLOTS * STEPS * HALF // (STEPS * HALF))
    routes = jax.vmap(lambda own, number: routed_block(jax.random.fold_in(streams_of[2], 2), own, number, STEPS * HALF, EXPERTS, TOPK, CAP_E, 2))(routes_keys, routes_turns).reshape((SLOTS, STEPS, HALF, TOPK))
    w_qkv = scatter_about(streams_of[3], (D, 3, HEADS * HDIM), D ** -0.5, 0.125, ((2, 4),))
    w_out = scatter_about(streams_of[4], (HEADS * HDIM, D), (HEADS * HDIM) ** -0.5, 0.125, ((0, 4),))
    prompt_keys = draw_prompt_keys(jax.random.fold_in(streams_of[14], 71), 0)
    prompt_values = scatter_about(streams_of[6], (SLOTS, CAP, HEADS * HDIM), 1.0, 6.0, ((0, 8), (2, 4)))
    prompt_parts = draw_prompt_parts(jax.random.fold_in(streams_of[14], 71), 0)
    tail_keys = scatter_about(streams_of[8], (SLOTS, HALF, PREV, HEADS * HDIM), 3.0, 18.0, ((0, 8), (3, 4)))
    tail_values = scatter_about(streams_of[9], (SLOTS, HALF, PREV, HEADS * HDIM), 1.0, 6.0, ((0, 8), (3, 4)))
    w_router = draw_w_router(jax.random.fold_in(streams_of[14], 71), 0)
    norm_gain = jnp.clip(1.0 + 0.18 * jax.random.normal(streams_of[11], (D,), jnp.float32), 0.1, 1.9)
    w_gate_up = scatter_about(streams_of[12], (EXPERTS, D, 2 * FFE), D ** -0.5, 0.125, ((0, 8), (1, 4)))
    w_down = scatter_about(streams_of[13], (EXPERTS, D, FFE), FFE ** -0.5, 0.15625, ((0, 8), (1, 4)))
    return dict(step_inputs=step_inputs, parents=parents, routes=routes, w_qkv=w_qkv, w_out=w_out, prompt_keys=prompt_keys, prompt_values=prompt_values, prompt_parts=prompt_parts, tail_keys=tail_keys, tail_values=tail_values, w_router=w_router, norm_gain=norm_gain, w_gate_up=w_gate_up, w_down=w_down)


NEGATIVE = -1e+30
EPSILON = 1e-06

def pair_steps(array):
    shape = array.shape
    paired = array.reshape((shape[0] // 2, 2) + shape[1:])
    paired = jnp.swapaxes(paired, 1, 2)
    return paired.reshape((shape[0] // 2, shape[1], 2 * shape[2]) + shape[3:])

def split_steps(array):
    shape = array.shape
    halves = array.reshape((shape[0], shape[1], 2, shape[2] // 2) + shape[3:])
    halves = jnp.swapaxes(halves, 1, 2)
    return halves.reshape((2 * shape[0], shape[1], shape[2] // 2) + shape[3:])

def attend_request(request_args, w_qkv):
    inputs_req, parents_req, keys_req, values_req, parts_req, tail_k_req, tail_v_req = request_args
    width = HEADS * HDIM
    packed = jnp.dot(inputs_req.reshape(STEPS * BEAMS, D), w_qkv.reshape(D, 3 * width), preferred_element_type=jnp.float32)
    packed = lax.optimization_barrier(packed.astype(jnp.bfloat16)).astype(jnp.float32)
    packed = packed.reshape(STEPS, BEAMS, 3, HEADS, HDIM)
    query_all = packed[:, :, 0]
    key_new = packed[:, :, 1]
    value_new = packed[:, :, 2]
    score_scale = HDIM ** (-0.5)
    prompt_keys_f = keys_req.reshape(2 * CAP, HEADS, HDIM).astype(jnp.float32)
    prompt_vals_f = values_req.reshape(2 * CAP, HEADS, HDIM).astype(jnp.float32)
    positions = jnp.arange(CAP, dtype=jnp.int32)
    live_pos = (positions[None, :] < parts_req[:, None]).reshape(2 * CAP)
    prompt_scores = jnp.einsum('sbhd,nhd->sbhn', query_all, prompt_keys_f, precision=lax.Precision.HIGHEST) * score_scale
    prompt_scores = jnp.where(live_pos, prompt_scores, NEGATIVE)
    tail_keys_f = jnp.zeros((BEAMS, TAIL, HEADS, HDIM), jnp.float32).at[:, :PREV].set(tail_k_req.reshape(BEAMS, PREV, HEADS, HDIM).astype(jnp.float32))
    tail_vals_f = jnp.zeros((BEAMS, TAIL, HEADS, HDIM), jnp.float32).at[:, :PREV].set(tail_v_req.reshape(BEAMS, PREV, HEADS, HDIM).astype(jnp.float32))
    tail_pos = jnp.arange(TAIL, dtype=jnp.int32)
    outputs = []
    for step_index in range(STEPS):
        tail_keys_f = tail_keys_f[parents_req[step_index]].at[:, PREV + step_index].set(key_new[step_index])
        tail_vals_f = tail_vals_f[parents_req[step_index]].at[:, PREV + step_index].set(value_new[step_index])
        tail_scores = jnp.einsum('bhd,bnhd->bhn', query_all[step_index], tail_keys_f, precision=lax.Precision.HIGHEST) * score_scale
        tail_scores = jnp.where(tail_pos <= PREV + step_index, tail_scores, NEGATIVE)
        joined = jnp.concatenate([prompt_scores[step_index], tail_scores], axis=2)
        best_top = lax.optimization_barrier(jnp.max(joined, axis=2, keepdims=True))
        weights = jnp.exp(joined - best_top)
        part_total = lax.optimization_barrier(jnp.sum(weights, axis=2))
        part_mix = jnp.einsum('bhn,nhd->bhd', weights[:, :, :2 * CAP], prompt_vals_f, precision=lax.Precision.HIGHEST)
        part_mix = part_mix + jnp.einsum('bhn,bnhd->bhd', weights[:, :, 2 * CAP:], tail_vals_f, precision=lax.Precision.HIGHEST)
        outputs.append((part_mix / part_total[:, :, None]).reshape(BEAMS, width))
    return jnp.stack(outputs).astype(jnp.bfloat16)

def expert_rows(expert_args):
    rows_in, gate_up, down = expert_args
    flat = rows_in.reshape(SLOTS * CAP_E, D)
    mixed_units = jnp.dot(flat, gate_up, preferred_element_type=jnp.float32)
    hidden_units = (jax.nn.silu(mixed_units[:, :FFE]) * mixed_units[:, FFE:]).astype(jnp.bfloat16)
    result = jnp.dot(hidden_units, down.T, preferred_element_type=jnp.float32).astype(jnp.bfloat16)
    return result.reshape(SLOTS, CAP_E, D)

def reference(step_inputs, parents, routes, w_qkv, w_out, prompt_keys, prompt_values, prompt_parts, tail_keys, tail_values, w_router, norm_gain, w_gate_up, w_down):
    requests = SLOTS // 2
    width = HEADS * HDIM
    request_args = (pair_steps(step_inputs), pair_steps(parents), prompt_keys.reshape(requests, 2, CAP, width), prompt_values.reshape(requests, 2, CAP, width), prompt_parts.reshape(requests, 2), tail_keys.reshape(requests, BEAMS, PREV, width), tail_values.reshape(requests, BEAMS, PREV, width))
    attended = lax.map(partial(attend_request, w_qkv=w_qkv), request_args)
    row_count = SLOTS * STEPS * HALF
    attention = split_steps(attended).reshape(row_count, width)
    residual_rows = step_inputs.reshape(row_count, D).astype(jnp.float32) + jnp.dot(attention, w_out, preferred_element_type=jnp.float32)
    mean_square = lax.optimization_barrier(jnp.mean(residual_rows * residual_rows, axis=1, keepdims=True))
    normed = (residual_rows * lax.rsqrt(mean_square + EPSILON) * norm_gain).astype(jnp.bfloat16)
    logits = jnp.dot(normed, w_router, preferred_element_type=jnp.float32)
    probs = jax.nn.softmax(logits, axis=1)
    chosen = routes.reshape(row_count, TOPK)
    picked = jnp.take_along_axis(probs, chosen, axis=1)
    route_share = picked / lax.optimization_barrier(jnp.sum(picked, axis=1, keepdims=True))
    entries = routes.reshape(SLOTS, STEPS * HALF * TOPK)
    route_match = (entries[:, :, None] == jnp.arange(EXPERTS, dtype=jnp.int32)[None, None, :]).astype(jnp.int32)
    earlier = (jnp.cumsum(route_match, axis=1) - route_match).astype(jnp.int32)
    slot_rank = lax.optimization_barrier(jnp.sum(route_match * earlier, axis=2)).astype(jnp.int32)
    slot_ids = jnp.broadcast_to(jnp.arange(SLOTS, dtype=jnp.int32)[:, None], entries.shape)
    repeated = jnp.repeat(normed.reshape(SLOTS, STEPS * HALF, D), TOPK, axis=1)
    dispatch = jnp.zeros((EXPERTS, SLOTS, CAP_E, D), jnp.bfloat16).at[entries, slot_ids, slot_rank].set(repeated)
    expert_out = lax.map(expert_rows, (dispatch, w_gate_up, w_down))
    fetched = expert_out[entries, slot_ids, slot_rank].astype(jnp.float32).reshape(row_count, TOPK, D)
    expert_mix = lax.optimization_barrier(jnp.sum(route_share[:, :, None] * fetched, axis=1))
    return (residual_rows + expert_mix).astype(jnp.bfloat16).reshape(SLOTS, STEPS, HALF, D)
```

```python
import functools

import jax
import jax.numpy as jnp
from jax import lax
from jax.experimental import pallas as pl
from jax.experimental.pallas import tpu as pltpu
from jax.sharding import PartitionSpec as P

HDIM = 128
EXPERTS = 64
FFE = 1408
TOPK = 6
BEAMS = 8
STEPS = 4
CAP_E = 3
HALF = 4
PREV = 60
LANES = 128
ROWS = STEPS * HALF
PAIR = 2 * ROWS
STATS = 1 + TOPK

NEGATIVE = -1e30
EPSILON = 1e-06
MIB = 1024 * 1024
BF = jnp.bfloat16
F32 = jnp.float32

VMEM = pl.BlockSpec(memory_space=pltpu.VMEM)
SMEM = pl.BlockSpec(memory_space=pltpu.SMEM)
ANY = pl.BlockSpec(memory_space=pl.ANY)


def iota(shape, dim):
    return lax.broadcasted_iota(jnp.int32, shape, dim)


def dot(a, b):
    return jnp.dot(a, b, preferred_element_type=F32)


def dot_t(a, b):
    return lax.dot_general(a, b, (((1,), (1,)), ((), ())), preferred_element_type=F32)


def t_dot(a, b):
    return lax.dot_general(a, b, (((0,), (0,)), ((), ())), preferred_element_type=F32)


def exchanged(value, axis, mask):
    pairs = [(source, source ^ mask) for source in range(lax.axis_size(axis))]
    return lax.ppermute(value, axis, pairs)


def call(body, outs, in_specs, *args, scratch=(), limit=32, flops=0, nbytes=0):
    return pl.pallas_call(
        body,
        out_shape=outs,
        in_specs=in_specs,
        out_specs=jax.tree.map(lambda _: VMEM, outs),
        scratch_shapes=list(scratch),
        compiler_params=pltpu.CompilerParams(vmem_limit_bytes=limit * MIB),
        cost_estimate=pl.CostEstimate(flops=flops, bytes_accessed=nbytes, transcendentals=0),
    )(*args)


def shape(dims, dtype):
    return jax.ShapeDtypeStruct(tuple(dims), dtype)


def attend_kernel(parts, par, x, wqkv, kp, vp, tk, tv, out):
    half = lax.axis_index("grp") % 2
    width = wqkv.shape[2]
    heads = width // HDIM
    rows = x[...]
    query = dot(rows, wqkv[0]).astype(BF)
    key_new = dot(rows, wqkv[1]).astype(BF)
    value_new = dot(rows, wqkv[2]).astype(BF)
    lane = iota((BEAMS, LANES), 1)
    beam = iota((BEAMS, LANES), 0)
    state = (lane == beam).astype(F32)
    states = []
    for step in range(STEPS):
        parent = par[:, step : step + 1]
        taken = jnp.zeros((BEAMS, LANES), F32)
        for j in range(BEAMS):
            taken = taken + jnp.where(parent == j, state[j : j + 1, :], 0.0)
        state = jnp.where(lane == BEAMS + BEAMS * step + beam, 1.0, taken)
        states.append(state)
    held = jnp.concatenate(states, axis=0).astype(BF)
    to_row = iota((PAIR, PAIR), 0)
    from_row = iota((PAIR, PAIR), 1)
    wanted = (to_row % ROWS // HALF) * BEAMS + (to_row // ROWS) * HALF + to_row % HALF
    held = dot((from_row == wanted).astype(BF), held).astype(BF)
    tails = tk.shape[0]
    place = iota((LANES, tails), 0)
    column = iota((LANES, tails), 1)
    tail_mask = dot(held, (place == half * HALF + column % HALF).astype(BF)) > 0.5
    place = iota((LANES, PAIR), 0)
    column = iota((LANES, PAIR), 1)
    new_at = BEAMS + BEAMS * (column % ROWS // HALF) + (column // ROWS) * HALF + column % HALF
    new_mask = dot(held, ((place == new_at) & (column // ROWS == half)).astype(BF)) > 0.5
    cap = kp.shape[0]
    live = iota((PAIR, cap), 1) < parts[0]
    scale = HDIM ** (-0.5)
    info = jnp.zeros((PAIR, LANES), F32)
    info_lane = iota((PAIR, LANES), 1)
    for head in range(heads):
        at = slice(head * HDIM, (head + 1) * HDIM)
        q = query[:, at]
        s_p = jnp.where(live, dot_t(q, kp[:, at]) * scale, NEGATIVE)
        s_t = jnp.where(tail_mask, dot_t(q, tk[:, at]) * scale, NEGATIVE)
        s_n = jnp.where(new_mask, dot_t(q, key_new[:, at]) * scale, NEGATIVE)
        top = jnp.maximum(
            jnp.max(s_p, axis=1, keepdims=True),
            jnp.maximum(
                jnp.max(s_t, axis=1, keepdims=True), jnp.max(s_n, axis=1, keepdims=True)
            ),
        )
        p_p = jnp.exp(s_p - top)
        p_t = jnp.exp(s_t - top)
        p_n = jnp.exp(s_n - top)
        total = (
            jnp.sum(p_p, axis=1, keepdims=True)
            + jnp.sum(p_t, axis=1, keepdims=True)
            + jnp.sum(p_n, axis=1, keepdims=True)
        )
        mix = (
            dot(p_p.astype(BF), vp[:, at])
            + dot(p_t.astype(BF), tv[:, at])
            + dot(p_n.astype(BF), value_new[:, at])
        )
        out[:, at] = mix
        info = jnp.where(info_lane == head, top, info)
        info = jnp.where(info_lane == heads + head, total, info)
    out[:, width:] = info


def project_kernel(near, far, w_out, *outs):
    me = lax.axis_index("exp")
    width = w_out.shape[0]
    heads = width // HDIM
    parts = []
    for head in range(heads):
        at = slice(head * HDIM, (head + 1) * HDIM)
        m_at = slice(width + head, width + head + 1)
        l_at = slice(width + heads + head, width + heads + head + 1)
        top = jnp.maximum(near[:, m_at], far[:, m_at])
        f_near = jnp.exp(near[:, m_at] - top)
        f_far = jnp.exp(far[:, m_at] - top)
        total = near[:, l_at] * f_near + far[:, l_at] * f_far
        mix = near[:, at] * f_near + far[:, at] * f_far
        parts.append((mix / total).astype(BF))
    attention = jnp.concatenate(parts, axis=1)
    features = outs[0].shape[1]
    for k, out in enumerate(outs):
        start = pl.multiple_of((me ^ k) * features, LANES)
        out[...] = dot(attention, w_out[:, pl.ds(start, features)]).astype(out.dtype)


def residual_kernel(x, gain, w_router, routes, own, *rest):
    others, (residual_out, message) = rest[:-2], rest[-2:]
    me = lax.axis_index("exp")
    features = own.shape[1]
    start = pl.multiple_of(me * features, LANES)
    residual = x[:, pl.ds(start, features)].astype(F32) + own[...]
    for other in others:
        residual = residual + other[...].astype(F32)
    residual_out[...] = residual
    rows = (residual * gain[...]).astype(BF)
    message[:, :features] = rows
    logits = dot(rows, w_router[...])
    expert = iota(logits.shape, 1)
    lane = iota((PAIR, LANES), 1)
    info = jnp.zeros((PAIR, LANES), F32)
    columns = [jnp.sum(residual * residual, axis=1, keepdims=True)]
    for k in range(TOPK):
        route = routes[:, k : k + 1]
        columns.append(jnp.sum(jnp.where(expert == route, logits, 0.0), axis=1, keepdims=True))
        info = jnp.where(lane == 2 * STATS + k, route.astype(F32), info)
    for at, column in enumerate(columns):
        high = column.astype(BF).astype(F32)
        info = jnp.where(lane == at, high, info)
        info = jnp.where(lane == STATS + at, column - high, info)
    message[:, features:] = info.astype(BF)


def gather_kernel(local, *refs):
    messages, (picked, stats, target, choice, rows) = refs[:-5], refs[-5:]
    blocks = len(messages)
    tokens = blocks * PAIR
    features = rows.shape[1]
    infos = []
    for k, message in enumerate(messages):
        rows[k * PAIR : (k + 1) * PAIR, :] = message[:, :features]
        infos.append(message[:, features:].astype(F32))
    info = jnp.concatenate(infos, axis=0).T
    stats[...] = jnp.concatenate(
        [info[:STATS] + info[STATS : 2 * STATS], jnp.zeros((8 - STATS, tokens), F32)], axis=0
    )
    first = (lax.axis_index("grp") * local).astype(F32)
    expert = iota((8, tokens), 0).astype(F32)
    chosen = jnp.full((8, tokens), -1.0, F32)
    for k in range(TOPK):
        route = info[2 * STATS + k : 2 * STATS + k + 1] - first
        chosen = jnp.where((route == expert) & (expert < local), float(k), chosen)
    choice[...] = chosen
    named = chosen >= 0.0
    before = iota((tokens, tokens), 0)
    after = iota((tokens, tokens), 1)
    earlier = ((before < after) & (before // ROWS == after // ROWS)).astype(BF)
    rank = dot(named.astype(BF), earlier)
    slot = (iota((8, tokens), 1) // ROWS).astype(F32)
    goal = jnp.where(named, slot * CAP_E + rank, -1.0)
    target[...] = goal
    capacity = picked.shape[0] // local
    row = iota((capacity, tokens), 0).astype(F32)
    places = [(row == goal[e : e + 1]).astype(BF) for e in range(local)]
    picked[...] = dot(jnp.concatenate(places, axis=0), rows[...]).astype(BF)


def gate_kernel(mask, block, has_far, keep, picked, weights, *refs):
    far = refs[0] if has_far else None
    out, buffer, sems = refs[-3:]
    me = lax.axis_index("exp")
    first = (me ^ mask) * block
    width = weights.shape[2] // 2
    copies = []
    for e in range(block):
        for part in range(2):
            at = pl.ds(part * width, width)
            copies.append(
                pltpu.make_async_copy(
                    weights.at[first + e, :, at], buffer.at[e, :, at], sems.at[2 * e + part]
                )
            )
    for copy in copies:
        copy.start()
    capacity = out.shape[0] // block
    start = pl.multiple_of(first * capacity, block * capacity)
    rows = picked[pl.ds(start, block * capacity), :]
    for part in range(2):
        sums = []
        for e in range(block):
            copies[2 * e + part].wait()
            sums.append(
                dot(
                    rows[e * capacity : (e + 1) * capacity],
                    buffer[e, :, part * width : (part + 1) * width],
                )
            )
        result = jnp.concatenate(sums, axis=0)
        at = slice(part * width, (part + 1) * width)
        if has_far:
            result = result + far[:, at].astype(F32)
        out[:, at] = result.astype(out.dtype)


def gate_block(mask, block, picked, weights, far, dtype):
    local, depth, width = weights.shape
    rows = picked.shape[0] // local * block
    args = (picked, weights) + (() if far is None else (far,))
    return call(
        functools.partial(gate_kernel, mask, block, far is not None, 0),
        shape((rows, width), dtype),
        [VMEM, ANY] + [VMEM] * (far is not None),
        *args,
        scratch=[
            pltpu.VMEM((block, depth, width), BF),
            pltpu.SemaphoreType.DMA((2 * block,)),
        ],
        flops=2 * rows * depth * width,
        nbytes=2 * block * depth * width,
    )


def hidden_kernel(block, near, far, target, stat0, stat1, stat2, stat3, hidden, total):
    me = lax.axis_index("exp")
    stats = (stat0[...] + stat1[...]) + (stat2[...] + stat3[...])
    total[...] = stats
    rows = near.shape[0]
    capacity = rows // block
    depth = 2048
    inverse = lax.rsqrt(stats[0:1] / depth + EPSILON)
    row = iota((capacity, target.shape[1]), 0).astype(F32)
    scales = []
    for e in range(block):
        goal = target[pl.ds(me * block + e, 1), :]
        scales.append(jnp.sum(jnp.where(row == goal, inverse, 0.0), axis=1, keepdims=True))
    scale = jnp.concatenate(scales, axis=0)
    width = near.shape[1] // 2
    gate = (near[:, :width] + far[:, :width].astype(F32)) * scale
    up = (near[:, width:] + far[:, width:].astype(F32)) * scale
    hidden[...] = (gate / (1.0 + jnp.exp(-gate)) * up).astype(BF)


def shares_of(stats):
    inverse = lax.rsqrt(stats[0:1] / 2048 + EPSILON)
    logits = [stats[1 + k : 2 + k] * inverse for k in range(TOPK)]
    top = functools.reduce(jnp.maximum, logits)
    weights = [jnp.exp(logit - top) for logit in logits]
    whole = functools.reduce(lambda a, b: a + b, weights)
    return [weight / whole for weight in weights]


def down_kernel(masks, block, mode, weights, stats, target, choice, *refs):
    count = len(masks)
    hiddens, refs = refs[:count], refs[count:]
    before = None
    if mode != "first":
        before, refs = refs[0], refs[1:]
    buffer, sems = refs[-2:]
    outs = refs[:-2]
    me = lax.axis_index("exp")
    copies = []
    for i, mask in enumerate(masks):
        for e in range(block):
            copies.append(
                pltpu.make_async_copy(
                    weights.at[(me ^ mask) * block + e],
                    buffer.at[i * block + e],
                    sems.at[i * block + e],
                )
            )
    for copy in copies:
        copy.start()
    shares = shares_of(stats[...])
    tokens = target.shape[1]
    capacity = hiddens[0].shape[0] // block
    row = iota((capacity, tokens), 0).astype(F32)
    places, results = [], []
    for i, mask in enumerate(masks):
        for e in range(block):
            at = (me ^ mask) * block + e
            goal = target[pl.ds(at, 1), :]
            picked = choice[pl.ds(at, 1), :]
            share = jnp.zeros((1, tokens), F32)
            for k in range(TOPK):
                share = jnp.where(picked == float(k), shares[k], share)
            places.append(jnp.where(row == goal, share, 0.0))
            copies[i * block + e].wait()
            units = hiddens[i][...].astype(F32)[e * capacity : (e + 1) * capacity].astype(BF)
            results.append(dot_t(units, buffer[i * block + e]))
    place = jnp.concatenate(places, axis=0)
    result = jnp.concatenate(results, axis=0).astype(BF)
    high = place.astype(BF)
    low = (place - high.astype(F32)).astype(BF)
    mixed = t_dot(high, result) + t_dot(low, result)
    if before is not None:
        mixed = mixed + before[...]
    if mode != "last":
        outs[0][...] = mixed
        return
    keep, send = outs
    half = lax.axis_index("grp") % 2
    for k in range(tokens // PAIR):
        low_rows = mixed[k * PAIR : k * PAIR + ROWS]
        high_rows = mixed[k * PAIR + ROWS : (k + 1) * PAIR]
        at = slice(k * ROWS, (k + 1) * ROWS)
        keep[at, :] = jnp.where(half == 0, low_rows, high_rows)
        send[at, :] = jnp.where(half == 0, high_rows, low_rows).astype(BF)


def down_blocks(masks, block, mode, weights, stats, target, choice, hiddens, before):
    features, width = weights.shape[1:]
    tokens = target.shape[1]
    if mode == "last":
        outs = (shape((tokens // 2, features), F32), shape((tokens // 2, features), BF))
    else:
        outs = (shape((tokens, features), F32),)
    args = (weights, stats, target, choice) + tuple(hiddens)
    if before is not None:
        args = args + (before,)
    experts = len(masks) * block
    return call(
        functools.partial(down_kernel, masks, block, mode),
        outs,
        [ANY] + [VMEM] * (len(args) - 1),
        *args,
        scratch=[
            pltpu.VMEM((experts, features, width), BF),
            pltpu.SemaphoreType.DMA((experts,)),
        ],
        flops=2 * experts * hiddens[0].shape[0] // block * features * width,
        nbytes=2 * experts * features * width,
    )


def fold_kernel(keep, far, *outs):
    for k, out in enumerate(outs):
        at = slice(k * ROWS, (k + 1) * ROWS)
        out[...] = (keep[at, :] + far[at, :].astype(F32)).astype(out.dtype)


def finish_kernel(residual, own, *rest):
    others, out = rest[:-1], rest[-1]
    half = lax.axis_index("grp") % 2
    value = residual[pl.ds(pl.multiple_of(half * ROWS, ROWS), ROWS), :] + own[...]
    for other in others:
        value = value + other[...].astype(F32)
    out[...] = value.astype(out.dtype)


def on_device(
    step_inputs,
    parents,
    routes,
    w_qkv,
    w_out,
    prompt_keys,
    prompt_values,
    prompt_parts,
    tail_keys,
    tail_values,
    w_router,
    norm_gain,
    w_gate_up,
    w_down,
):
    groups = lax.axis_size("grp")
    splits = lax.axis_size("exp")
    requests = groups // 2
    low_first = lax.axis_index("grp") % 2 == 0
    model = w_qkv.shape[0]
    width = w_qkv.shape[2]
    features = norm_gain.shape[0]
    local = w_gate_up.shape[0]
    tokens = requests * PAIR

    def both(own, other, dims):
        own, other = own.reshape(dims), other.reshape(dims)
        return jnp.concatenate(
            [jnp.where(low_first, own, other), jnp.where(low_first, other, own)], axis=0
        )

    own_inputs, own_parents, own_routes = step_inputs[0], parents[0], routes[0]
    far_inputs, far_parents, far_routes = exchanged(
        (own_inputs, own_parents, own_routes), "grp", 1
    )
    x = both(own_inputs, far_inputs, (ROWS, model))
    routes_all = both(own_routes, far_routes, (ROWS, TOPK))
    par = both(own_parents.T, far_parents.T, (HALF, STEPS))
    tail_k = tail_keys[0].transpose(1, 0, 2).reshape(PREV * HALF, width)
    tail_v = tail_values[0].transpose(1, 0, 2).reshape(PREV * HALF, width)
    near = call(
        attend_kernel,
        shape((PAIR, width + LANES), F32),
        [SMEM] + [VMEM] * 7,
        prompt_parts,
        par,
        x,
        w_qkv.transpose(1, 0, 2),
        prompt_keys[0],
        prompt_values[0],
        tail_k,
        tail_v,
        flops=2 * PAIR * model * 3 * width,
        nbytes=6 * model * width,
    )
    far = exchanged(near, "grp", 1)
    terms = call(
        project_kernel,
        tuple(shape((PAIR, features), F32 if k == 0 else BF) for k in range(splits)),
        [VMEM] * 3,
        near,
        far,
        w_out,
        flops=2 * PAIR * width * model,
        nbytes=2 * width * model,
    )
    arrived = [exchanged(terms[k], "exp", k) for k in range(1, splits)]
    residual, message = call(
        residual_kernel,
        (shape((PAIR, features), F32), shape((PAIR, features + LANES), BF)),
        [VMEM] * (5 + len(arrived)),
        x,
        norm_gain.reshape(1, features),
        w_router,
        routes_all,
        terms[0],
        *arrived,
    )
    messages = [message] + [exchanged(message, "grp", 2 * k) for k in range(1, requests)]
    picked, stats, target, choice = call(
        functools.partial(gather_kernel, local),
        (
            shape((EXPERTS * CAP_E, features), BF),
            shape((8, tokens), F32),
            shape((8, tokens), F32),
            shape((8, tokens), F32),
        ),
        [VMEM] * requests,
        *messages,
        scratch=[pltpu.VMEM((tokens, features), BF)],
    )
    if splits == 4 and local % splits == 0:
        block = local // splits
        gate = functools.partial(gate_block, block=block, picked=picked, weights=w_gate_up)
        far_stats = [exchanged(stats, "exp", k) for k in range(1, splits)]
        sums_a = gate(3, far=None, dtype=BF)
        far_a = exchanged(sums_a, "exp", 1)
        sums_b = gate(1, far=None, dtype=BF)
        sums_c = gate(2, far=far_a, dtype=BF)
        far_b = exchanged(sums_b, "exp", 1)
        far_c = exchanged(sums_c, "exp", 2)
        sums_d = gate(0, far=far_b, dtype=F32)
        hidden, stats = call(
            functools.partial(hidden_kernel, block),
            (shape((sums_d.shape[0], FFE), BF), shape((8, tokens), F32)),
            [VMEM] * 7,
            sums_d,
            far_c,
            target,
            stats,
            *far_stats,
        )
        down = functools.partial(
            down_blocks, block=block, weights=w_down, stats=stats, target=target, choice=choice
        )
        hidden_y = exchanged(hidden, "exp", 2)
        hidden_c = exchanged(hidden, "exp", 1)
        hidden_f = exchanged(hidden_y, "exp", 1)
        (mixed,) = down((0, 1), mode="first", hiddens=(hidden, hidden_c), before=None)
        (mixed,) = down((2,), mode="more", hiddens=(hidden_y,), before=mixed)
        keep, send = down((3,), mode="last", hiddens=(hidden_f,), before=mixed)
    else:
        stats = lax.psum(stats, "exp")
        rows = picked.reshape(local, -1, features)
        sums = jnp.einsum("lcd,ldf->lcf", rows, w_gate_up, preferred_element_type=F32)
        sums = lax.psum(sums.astype(BF), "exp").astype(F32)
        inverse = lax.rsqrt(stats[0] / model + EPSILON)
        goal, pick = target[:local], choice[:local]
        place = goal[:, None, :] == jnp.arange(rows.shape[1], dtype=F32)[None, :, None]
        sums = sums * jnp.sum(jnp.where(place, inverse, 0.0), axis=2, keepdims=True)
        hidden = (jax.nn.silu(sums[..., :FFE]) * sums[..., FFE:]).astype(BF)
        result = jnp.einsum("lcf,ldf->lcd", hidden, w_down, preferred_element_type=F32)
        share = jax.nn.softmax(stats[1:STATS] * inverse, axis=0)
        ids = jnp.arange(TOPK, dtype=F32)[None, :, None]
        weight = jnp.sum(jnp.where(pick[:, None, :] == ids, share[None], 0.0), axis=1)
        mixed = jnp.einsum(
            "lct,lcd->td",
            jnp.where(place, weight[:, None, :], 0.0),
            result.astype(BF).astype(F32),
            precision=lax.Precision.HIGHEST,
        ).reshape(requests, 2, ROWS, features)
        pair_half = lax.axis_index("grp") % 2
        keep = lax.dynamic_index_in_dim(mixed, pair_half, 1, False).reshape(-1, features)
        send = lax.dynamic_index_in_dim(mixed, 1 - pair_half, 1, False)
        send = send.reshape(-1, features).astype(BF)
    folded = call(
        fold_kernel,
        tuple(shape((ROWS, features), F32 if k == 0 else BF) for k in range(requests)),
        [VMEM] * 2,
        keep,
        exchanged(send, "grp", 1),
    )
    back = [exchanged(folded[k], "grp", 2 * k) for k in range(1, requests)]
    result = call(
        finish_kernel,
        shape((ROWS, features), BF),
        [VMEM] * (2 + len(back)),
        residual,
        folded[0],
        *back,
    )
    return result.reshape(1, STEPS, HALF, features)


def solution(mesh):
    placed = (
        P("grp", None, None, None),
        P("grp", None, None),
        P("grp", None, None, None),
        P(None, None, "exp"),
        P("exp", None),
        P("grp", None, "exp"),
        P("grp", None, "exp"),
        P("grp"),
        P("grp", None, None, "exp"),
        P("grp", None, None, "exp"),
        P("exp", None),
        P("exp"),
        P("grp", "exp", None),
        P("grp", "exp", None),
    )
    return jax.shard_map(
        on_device,
        mesh=mesh,
        in_specs=placed,
        out_specs=P("grp", None, None, "exp"),
        check_vma=False,
    )
```

```python
import functools

import jax
import jax.numpy as jnp
from jax import lax
from jax.experimental import pallas as pl
from jax.experimental.pallas import tpu as pltpu
from jax.sharding import PartitionSpec as P

HDIM = 128
EXPERTS = 64
FFE = 1408
TOPK = 6
BEAMS = 8
STEPS = 4
CAP_E = 3
HALF = 4
PREV = 60
LANES = 128
MODEL = 2048
ROWS = STEPS * HALF
PAIR = 2 * ROWS
STATS = 1 + TOPK

NEGATIVE = -1e30
EPSILON = 1e-06
MIB = 1024 * 1024
BF = jnp.bfloat16
HINT = 10**10
F32 = jnp.float32

VMEM = pl.BlockSpec(memory_space=pltpu.VMEM)
SMEM = pl.BlockSpec(memory_space=pltpu.SMEM)
ANY = pl.BlockSpec(memory_space=pl.ANY)


def iota(shape, dim):
    return lax.broadcasted_iota(jnp.int32, shape, dim)


def dot(a, b):
    return jnp.dot(a, b, preferred_element_type=F32)


def dot_t(a, b):
    return lax.dot_general(a, b, (((1,), (1,)), ((), ())), preferred_element_type=F32)


def t_dot(a, b):
    return lax.dot_general(a, b, (((0,), (0,)), ((), ())), preferred_element_type=F32)


def exchanged(value, axis, mask):
    pairs = [(source, source ^ mask) for source in range(lax.axis_size(axis))]
    return lax.ppermute(value, axis, pairs)


def call(body, outs, in_specs, *args, after=(), scratch=(), limit=8, flops=0, nbytes=0):
    count = len(args)

    def ordered(*refs):
        body(*refs[:count], *refs[count + len(after) :])

    return pl.pallas_call(
        ordered if after else body,
        out_shape=outs,
        in_specs=list(in_specs) + [ANY] * len(after),
        out_specs=jax.tree.map(lambda _: VMEM, outs),
        scratch_shapes=list(scratch),
        compiler_params=pltpu.CompilerParams(vmem_limit_bytes=limit * MIB),
        cost_estimate=pl.CostEstimate(flops=flops, bytes_accessed=nbytes, transcendentals=0),
    )(*args, *after)


def shape(dims, dtype):
    return jax.ShapeDtypeStruct(tuple(dims), dtype)


def columns_kernel(order, tail_at, new_at):
    half = lax.axis_index("grp") % 2
    to_row = iota(order.shape, 0)
    wanted = (to_row % ROWS // HALF) * BEAMS + (to_row // ROWS) * HALF + to_row % HALF
    order[...] = (iota(order.shape, 1) == wanted).astype(BF)
    column = iota(tail_at.shape, 1)
    tail_at[...] = (iota(tail_at.shape, 0) == half * HALF + column % HALF).astype(BF)
    column = iota(new_at.shape, 1)
    beam = (column // ROWS) * HALF + column % HALF
    place = BEAMS + BEAMS * (column % ROWS // HALF) + beam
    here = (iota(new_at.shape, 0) == place) & (column // ROWS == half)
    new_at[...] = here.astype(BF)


def slot_rows(source):
    return jnp.concatenate([source[step].astype(F32) for step in range(STEPS)], axis=0)


def in_order(first, own, far):
    return jnp.concatenate([jnp.where(first, own, far), jnp.where(first, far, own)], axis=0)


def pieces(value, count):
    out = []
    for _ in range(count - 1):
        out.append(value.astype(BF).astype(F32))
        value = value - out[-1]
    return out + [value]


def attend_kernel(
    parts,
    order,
    tail_at,
    new_at,
    par_own,
    par_far,
    routes,
    x_own,
    x_far,
    wqkv,
    kp,
    vp,
    tk_raw,
    tv_raw,
    out,
    x_out,
):
    half = lax.axis_index("grp") % 2
    width = wqkv.shape[2]
    heads = width // HDIM
    x_all = in_order(half == 0, slot_rows(x_own), slot_rows(x_far))
    rows = x_all.astype(BF)
    features = x_out.shape[1]
    me = lax.axis_index("exp")
    mine = jnp.zeros((PAIR, features), F32)
    for k in range(x_all.shape[1] // features):
        mine = jnp.where(me == k, x_all[:, k * features : (k + 1) * features], mine)
    x_out[...] = mine
    query = dot(rows, wqkv[0]).astype(BF)
    key_new = dot(rows, wqkv[1]).astype(BF)
    value_new = dot(rows, wqkv[2]).astype(BF)
    lane = iota((BEAMS, LANES), 1)
    beam = iota((BEAMS, LANES), 0)
    state = (lane == beam).astype(F32)
    states = []
    same = iota((HALF, HALF), 0) == iota((HALF, HALF), 1)
    for step in range(STEPS):
        columns = [
            jnp.sum(
                jnp.where(same, source[step : step + 1, :].astype(F32), 0.0),
                axis=1,
                keepdims=True,
            )
            for source in (par_own, par_far)
        ]
        parent = in_order(half == 0, *columns)
        taken = jnp.zeros((BEAMS, LANES), F32)
        for j in range(BEAMS):
            taken = taken + jnp.where(parent == float(j), state[j : j + 1, :], 0.0)
        state = jnp.where(lane == BEAMS + BEAMS * step + beam, 1.0, taken)
        states.append(state)
    held = jnp.concatenate(states, axis=0).astype(BF)
    held = dot(order[...], held).astype(BF)
    tail_mask = dot(held, tail_at[...]) > 0.5
    new_mask = dot(held, new_at[...]) > 0.5
    tk = tk_raw[...].reshape(PREV * HALF, width)
    tv = tv_raw[...].reshape(PREV * HALF, width)
    cap = kp.shape[0]
    live = iota((PAIR, cap), 1) < parts[0]
    scale = HDIM ** (-0.5)
    info = jnp.zeros((PAIR, LANES), F32)
    info_lane = iota((PAIR, LANES), 1)
    own_rows = iota((PAIR, LANES), 0) // ROWS == half
    named = slot_rows(routes)
    named = jnp.concatenate([named, named], axis=0)
    for k in range(TOPK):
        info = jnp.where((info_lane == 5 * heads + k) & own_rows, named[:, k : k + 1], info)
    for head in range(heads):
        at = slice(head * HDIM, (head + 1) * HDIM)
        q = query[:, at]
        s_p = jnp.where(live, dot_t(q, kp[:, at]) * scale, NEGATIVE)
        s_t = jnp.where(tail_mask, dot_t(q, tk[:, at]) * scale, NEGATIVE)
        s_n = jnp.where(new_mask, dot_t(q, key_new[:, at]) * scale, NEGATIVE)
        top = jnp.maximum(
            jnp.max(s_p, axis=1, keepdims=True),
            jnp.maximum(
                jnp.max(s_t, axis=1, keepdims=True), jnp.max(s_n, axis=1, keepdims=True)
            ),
        )
        p_p = jnp.exp(s_p - top)
        p_t = jnp.exp(s_t - top)
        p_n = jnp.exp(s_n - top)
        total = (
            jnp.sum(p_p, axis=1, keepdims=True)
            + jnp.sum(p_t, axis=1, keepdims=True)
            + jnp.sum(p_n, axis=1, keepdims=True)
        )
        mix = (
            dot(p_p.astype(BF), vp[:, at])
            + dot(p_t.astype(BF), tv[:, at])
            + dot(p_n.astype(BF), value_new[:, at])
        )
        out[:, at] = mix.astype(BF)
        for k, column in enumerate(pieces(top, 3) + pieces(total, 2)):
            info = jnp.where(info_lane == k * heads + head, column, info)
    out[:, width:] = info.astype(BF)


def project_kernel(near, far, w_out, *outs):
    me = lax.axis_index("exp")
    width = w_out.shape[0]
    heads = width // HDIM
    parts = []
    infos = [side[:, width:].astype(F32) for side in (near, far)]
    for head in range(heads):
        at = slice(head * HDIM, (head + 1) * HDIM)
        columns = [
            [info[:, k * heads + head : k * heads + head + 1] for k in range(5)] for info in infos
        ]
        (m_near, l_near), (m_far, l_far) = [
            ((c[0] + c[1]) + c[2], c[3] + c[4]) for c in columns
        ]
        top = jnp.maximum(m_near, m_far)
        f_near = jnp.exp(m_near - top)
        f_far = jnp.exp(m_far - top)
        total = l_near * f_near + l_far * f_far
        mix = near[:, at].astype(F32) * f_near + far[:, at].astype(F32) * f_far
        parts.append((mix / total).astype(BF))
    attention = jnp.concatenate(parts, axis=1)
    features = outs[0].shape[1]
    for k, out in enumerate(outs):
        start = pl.multiple_of((me ^ k) * features, LANES)
        out[...] = dot(attention, w_out[:, pl.ds(start, features)]).astype(out.dtype)


def residual_kernel(x, gain, w_router, near, far, own, *rest):
    others, (residual_out, message) = rest[:-2], rest[-2:]
    features = own.shape[1]
    width = near.shape[1] - LANES
    named = near[:, width:].astype(F32) + far[:, width:].astype(F32)
    routes_at = 5 * (width // HDIM)
    residual = x[...] + own[...]
    for other in others:
        residual = residual + other[...].astype(F32)
    residual_out[...] = residual
    rows = (residual * gain[...]).astype(BF)
    message[:, :features] = rows
    logits = dot_t(rows, w_router[...])
    expert = iota(logits.shape, 1).astype(F32)
    lane = iota((PAIR, LANES), 1)
    info = jnp.zeros((PAIR, LANES), F32)
    columns = [jnp.sum(residual * residual, axis=1, keepdims=True)]
    for k in range(TOPK):
        route = named[:, routes_at + k : routes_at + k + 1]
        columns.append(jnp.sum(jnp.where(expert == route, logits, 0.0), axis=1, keepdims=True))
        info = jnp.where(lane == 2 * STATS + k, route, info)
    for at, column in enumerate(columns):
        high = column.astype(BF).astype(F32)
        info = jnp.where(lane == at, high, info)
        info = jnp.where(lane == STATS + at, column - high, info)
    message[:, features:] = info.astype(BF)


def gather_kernel(local, *refs):
    messages, (picked, stats, target, choice, rows) = refs[:-5], refs[-5:]
    blocks = len(messages)
    tokens = blocks * PAIR
    features = rows.shape[1]
    infos = []
    for k, message in enumerate(messages):
        rows[k * PAIR : (k + 1) * PAIR, :] = message[:, :features]
        infos.append(message[:, features:].astype(F32))
    info = jnp.concatenate(infos, axis=0).T
    stats[...] = jnp.concatenate(
        [info[:STATS] + info[STATS : 2 * STATS], jnp.zeros((8 - STATS, tokens), F32)], axis=0
    )
    first = (lax.axis_index("grp") * local).astype(F32)
    expert = iota((8, tokens), 0).astype(F32)
    chosen = jnp.full((8, tokens), -1.0, F32)
    for k in range(TOPK):
        route = info[2 * STATS + k : 2 * STATS + k + 1] - first
        chosen = jnp.where((route == expert) & (expert < local), float(k), chosen)
    choice[...] = chosen
    named = chosen >= 0.0
    before = iota((tokens, tokens), 0)
    after = iota((tokens, tokens), 1)
    earlier = ((before < after) & (before // ROWS == after // ROWS)).astype(BF)
    rank = dot(named.astype(BF), earlier)
    slot = (iota((8, tokens), 1) // ROWS).astype(F32)
    goal = jnp.where(named, slot * CAP_E + rank, -1.0)
    target[...] = goal
    capacity = picked.shape[1]
    row = iota((capacity, tokens), 0).astype(F32)
    places = [(row == goal[e : e + 1]).astype(F32) for e in range(local)]
    result = dot(jnp.concatenate(places, axis=0).astype(BF), rows[...])
    for e in range(local):
        picked[e] = result[e * capacity : (e + 1) * capacity].astype(BF)


def split_rows(value, rows):
    high = value[:STATS].astype(BF).astype(F32)
    low = value[:STATS] - high
    rest = jnp.zeros((rows - 2 * STATS, value.shape[1]), F32)
    return jnp.concatenate([high, low, rest], axis=0).astype(BF)


def joined_rows(value):
    value = value.astype(F32)
    high, low = value[:STATS], value[STATS : 2 * STATS]
    return jnp.concatenate([high + low, jnp.zeros((8 - STATS, value.shape[1]), F32)], axis=0)


def gate_kernel(places, block, with_stats, count, weights, picked, *refs):
    if with_stats:
        stats, refs = refs[0], refs[1:]
    far, outs = refs[:count], refs[count:]
    me = lax.axis_index("exp")
    width = weights.shape[2]
    for i, (mask, pick) in enumerate(places):
        at = (me ^ mask) * block + pick
        result = dot(picked[at], weights[at])
        if far:
            result = result + far[i][:, :width].astype(F32)
        outs[i][:, :width] = result.astype(outs[i].dtype)
    if with_stats:
        value = stats[...]
        if far:
            value = value + joined_rows(far[0][:, width:])
            outs[-1][...] = value
        outs[0][:, width:] = split_rows(value, outs[0].shape[0])


def gate_block(places, weights, picked, block, stats=(), far=(), dtypes=(BF,), after=(), flops=0):
    capacity, depth = picked.shape[1:]
    width = weights.shape[2]
    outs = [shape((capacity, width), dtype) for dtype in dtypes]
    if stats:
        outs[0] = shape((capacity, width + stats[0].shape[1]), BF)
        if far:
            outs.append(shape(stats[0].shape, F32))
    return call(
        functools.partial(gate_kernel, places, block, bool(stats), len(far)),
        tuple(outs),
        [VMEM] * (2 + len(stats) + len(far)),
        weights,
        picked,
        *stats,
        *far,
        after=after,
        flops=flops,
    )


def place_kernel(local, target, choice, stats, far, high, low):
    stats = stats[...] + joined_rows(far[:, far.shape[1] - target.shape[1] :])
    inverse = lax.rsqrt(stats[0:1] / MODEL + EPSILON)
    logits = [stats[1 + k : 2 + k] * inverse for k in range(TOPK)]
    top = functools.reduce(jnp.maximum, logits)
    weights = [jnp.exp(logit - top) for logit in logits]
    whole = functools.reduce(lambda a, b: a + b, weights)
    chosen = choice[...]
    share = jnp.zeros(chosen.shape, F32)
    for k in range(TOPK):
        share = jnp.where(chosen == float(k), weights[k] / whole, share)
    row = iota(high.shape[1:], 0).astype(F32)
    for e in range(local):
        place = jnp.where(row == target[e : e + 1, :], share[e : e + 1], 0.0)
        rounded = place.astype(BF)
        high[e] = rounded
        low[e] = (place - rounded.astype(F32)).astype(BF)


def hidden_kernel(block, pick, near, mid, far, target, stats, far_stats, hidden):
    capacity = near.shape[0]
    stats = stats[...] + joined_rows(far_stats[:, far_stats.shape[1] - target.shape[1] :])
    inverse = lax.rsqrt(stats[0:1] / MODEL + EPSILON)
    goal = target[pl.ds(lax.axis_index("exp") * block + pick, 1), :]
    row = iota((capacity, target.shape[1]), 0).astype(F32)
    scale = jnp.sum(jnp.where(row == goal, inverse, 0.0), axis=1, keepdims=True)
    half = near.shape[1] // 2
    gate = near[:, :half] + mid[:, :half].astype(F32) + far[:, :half].astype(F32)
    up = near[:, half:] + mid[:, half:].astype(F32) + far[:, half : 2 * half].astype(F32)
    gate, up = gate * scale, up * scale
    hidden[...] = (gate / (1.0 + jnp.exp(-gate)) * up).astype(BF)


def down_kernel(places, block, last, count, weights, high, low, *refs):
    hiddens, refs = refs[: len(places)], refs[len(places) :]
    before, refs = refs[:count], refs[count:]
    me = lax.axis_index("exp")
    mixed = before[0][...] if before else 0.0
    for hidden, (mask, pick) in zip(hiddens, places):
        at = (me ^ mask) * block + pick
        result = dot_t(hidden[...], weights[at]).astype(BF)
        mixed = mixed + (t_dot(high[at], result) + t_dot(low[at], result))
    if not last:
        refs[0][...] = mixed
        return
    send, rows = refs
    rows[...] = mixed
    request = lax.axis_index("grp") // 2
    for group in range(send.shape[0]):
        start = ((group // 2) ^ request) * PAIR + group % 2 * ROWS
        send[group] = rows[pl.ds(pl.multiple_of(start, ROWS), ROWS), :].astype(BF)


def down_blocks(places, hiddens, weights, high, low, block, before=(), last=False, after=()):
    features, width = weights.shape[1:]
    tokens = high.shape[2]
    if last:
        out = shape((tokens // ROWS, ROWS, features), BF)
    else:
        out = shape((tokens, features), F32)
    return call(
        functools.partial(down_kernel, places, block, last, len(before)),
        out,
        [VMEM] * (3 + len(hiddens) + len(before)),
        weights,
        high,
        low,
        *hiddens,
        *before,
        after=after,
        scratch=[pltpu.VMEM((tokens, features), F32)] if last else [],
    )


def finish_kernel(residual, back, out):
    half = lax.axis_index("grp") % 2
    value = residual[pl.ds(pl.multiple_of(half * ROWS, ROWS), ROWS), :]
    for group in range(back.shape[0]):
        value = value + back[group].astype(F32)
    out[...] = value.astype(out.dtype)


def on_device(
    step_inputs,
    parents,
    routes,
    w_qkv,
    w_out,
    prompt_keys,
    prompt_values,
    prompt_parts,
    tail_keys,
    tail_values,
    w_router,
    norm_gain,
    w_gate_up,
    w_down,
):
    groups = lax.axis_size("grp")
    splits = lax.axis_size("exp")
    requests = groups // 2
    model = w_qkv.shape[0]
    width = w_qkv.shape[2]
    features = norm_gain.shape[0]
    local = w_gate_up.shape[0]
    tokens = requests * PAIR

    columns = call(
        columns_kernel,
        (
            shape((PAIR, PAIR), BF),
            shape((LANES, PREV * HALF), BF),
            shape((LANES, PAIR), BF),
        ),
        [],
        flops=HINT,
    )
    own_inputs, own_parents, columns = lax.optimization_barrier(
        (step_inputs[0], parents[0], columns)
    )
    far_inputs, far_parents = exchanged((own_inputs, own_parents), "grp", 1)
    near, x = call(
        attend_kernel,
        (shape((PAIR, width + LANES), BF), shape((PAIR, features), F32)),
        [SMEM] + [VMEM] * 13,
        prompt_parts,
        *columns,
        parents[0],
        far_parents,
        routes[0],
        step_inputs[0],
        far_inputs,
        w_qkv.transpose(1, 0, 2),
        prompt_keys[0],
        prompt_values[0],
        tail_keys[0].transpose(1, 0, 2),
        tail_values[0].transpose(1, 0, 2),
        flops=HINT,
    )
    far = exchanged(near, "grp", 1)
    terms = call(
        project_kernel,
        tuple(shape((PAIR, features), F32 if k == 0 else BF) for k in range(splits)),
        [VMEM] * 3,
        near,
        far,
        w_out,
        flops=HINT,
    )
    arrived = [exchanged(terms[k], "exp", k) for k in range(1, splits)]
    residual, message = call(
        residual_kernel,
        (shape((PAIR, features), F32), shape((PAIR, features + LANES), BF)),
        [VMEM] * (6 + len(arrived)),
        x,
        norm_gain.reshape(1, features),
        w_router.T,
        near,
        far,
        terms[0],
        *arrived,
        flops=HINT,
    )
    messages = [message] + [exchanged(message, "grp", 2 * k) for k in range(1, requests)]
    picked, stats, target, choice = call(
        functools.partial(gather_kernel, local),
        (
            shape((local, EXPERTS * CAP_E // local, features), BF),
            shape((8, tokens), F32),
            shape((8, tokens), F32),
            shape((8, tokens), F32),
        ),
        [VMEM] * requests,
        *messages,
        scratch=[pltpu.VMEM((tokens, features), BF)],
        flops=HINT,
    )
    if splits == 4 and local == 2 * splits:
        gate = functools.partial(gate_block, weights=w_gate_up, picked=picked, block=2)
        (a0,) = gate(((3, 0),), stats=(stats,))
        far_a0 = exchanged(a0, "exp", 1)
        (a1,) = gate(((3, 1),), after=(a0,))
        far_a1 = exchanged(a1, "exp", 1)
        c0, stats = gate(((2, 0),), stats=(stats,), far=(far_a0,), after=(a1,))
        far_c0 = exchanged(c0, "exp", 2)
        (c1,) = gate(((2, 1),), far=(far_a1,), after=(c0,))
        far_c1 = exchanged(c1, "exp", 2)
        b0, b1, d0, d1 = gate(
            ((1, 0), (1, 1), (0, 0), (0, 1)), dtypes=(BF, BF, F32, F32), after=(c1,), flops=HINT // 2
        )
        far_b0, far_b1 = exchanged((b0, b1), "exp", 1)

        def hidden_of(pick, near, mid, far, after=()):
            return call(
                functools.partial(hidden_kernel, 2, pick),
                shape((near.shape[0], FFE), BF),
                [VMEM] * 6,
                near,
                mid,
                far,
                target,
                stats,
                far_c0,
                after=after,
                flops=HINT // 2,
            )

        own0 = hidden_of(0, d0, far_b0, far_c0)
        core0 = exchanged(own0, "exp", 1)
        y0 = exchanged(own0, "exp", 2)
        place = shape((local, picked.shape[1], tokens), BF)
        high, low = call(
            functools.partial(place_kernel, local),
            (place, place),
            [VMEM] * 4,
            target,
            choice,
            stats,
            far_c0,
            after=(own0,),
        )
        down = functools.partial(down_blocks, weights=w_down, high=high, low=low, block=2)
        mixed = down(((0, 0), (1, 0)), (own0, core0))
        own1 = hidden_of(1, d1, far_b1, far_c1, after=(mixed,))
        core1 = exchanged(own1, "exp", 1)
        y1 = exchanged(own1, "exp", 2)
        mixed = down(((0, 1), (1, 1)), (own1, core1), before=(mixed,))
        far0 = exchanged(y0, "exp", 1)
        mixed = down(((2, 0),), (y0,), before=(mixed,))
        y1, mixed = lax.optimization_barrier((y1, mixed))
        far1 = exchanged(y1, "exp", 1)
        mixed = down(((2, 1), (3, 0)), (y1, far0), before=(mixed,))
        send = down(((3, 1),), (far1,), before=(mixed,), last=True)
    else:
        stats = lax.psum(stats, "exp")
        sums = jnp.einsum("lcd,ldf->lcf", picked, w_gate_up, preferred_element_type=F32)
        sums = lax.psum(sums.astype(BF), "exp").astype(F32)
        inverse = lax.rsqrt(stats[0] / model + EPSILON)
        goal, pick = target[:local], choice[:local]
        place = goal[:, None, :] == jnp.arange(picked.shape[1], dtype=F32)[None, :, None]
        sums = sums * jnp.sum(jnp.where(place, inverse, 0.0), axis=2, keepdims=True)
        hidden = (jax.nn.silu(sums[..., :FFE]) * sums[..., FFE:]).astype(BF)
        result = jnp.einsum("lcf,ldf->lcd", hidden, w_down, preferred_element_type=F32)
        share = jax.nn.softmax(stats[1:STATS] * inverse, axis=0)
        ids = jnp.arange(TOPK, dtype=F32)[None, :, None]
        weight = jnp.sum(jnp.where(pick[:, None, :] == ids, share[None], 0.0), axis=1)
        mixed = jnp.einsum(
            "lct,lcd->td",
            jnp.where(place, weight[:, None, :], 0.0),
            result.astype(BF).astype(F32),
            precision=lax.Precision.HIGHEST,
        ).reshape(requests, 2 * ROWS, features)
        order = jnp.arange(requests) ^ (lax.axis_index("grp") // 2)
        send = mixed[order].reshape(groups, ROWS, features).astype(BF)
    back = lax.all_to_all(send, "grp", split_axis=0, concat_axis=0, tiled=True)
    result = call(
        finish_kernel, shape((ROWS, features), BF), [VMEM] * 2, residual, back
    )
    return result.reshape(1, STEPS, HALF, features)


def solution(mesh):
    placed = (
        P("grp", None, None, None),
        P("grp", None, None),
        P("grp", None, None, None),
        P(None, None, "exp"),
        P("exp", None),
        P("grp", None, "exp"),
        P("grp", None, "exp"),
        P("grp"),
        P("grp", None, None, "exp"),
        P("grp", None, None, "exp"),
        P("exp", None),
        P("exp"),
        P("grp", "exp", None),
        P("grp", "exp", None),
    )
    return jax.shard_map(
        on_device,
        mesh=mesh,
        in_specs=placed,
        out_specs=P("grp", None, None, "exp"),
        check_vma=False,
    )
```

```python
import functools

import jax
import jax.numpy as jnp
from jax import lax
from jax.experimental import pallas as pl
from jax.experimental.pallas import tpu as pltpu
from jax.sharding import PartitionSpec as P

HDIM = 128
EXPERTS = 64
FFE = 1408
TOPK = 6
BEAMS = 8
STEPS = 4
CAP_E = 3
HALF = 4
PREV = 60
LANES = 128
MODEL = 2048
ROWS = STEPS * HALF
PAIR = 2 * ROWS
STATS = 1 + TOPK

NEGATIVE = -1e30
EPSILON = 1e-06
MIB = 1024 * 1024
BF = jnp.bfloat16
HINT = 10**10
F32 = jnp.float32

VMEM = pl.BlockSpec(memory_space=pltpu.VMEM)
SMEM = pl.BlockSpec(memory_space=pltpu.SMEM)
ANY = pl.BlockSpec(memory_space=pl.ANY)


def iota(shape, dim):
    return lax.broadcasted_iota(jnp.int32, shape, dim)


def dot(a, b):
    return jnp.dot(a, b, preferred_element_type=F32)


def dot_t(a, b):
    return lax.dot_general(a, b, (((1,), (1,)), ((), ())), preferred_element_type=F32)


def t_dot(a, b):
    return lax.dot_general(a, b, (((0,), (0,)), ((), ())), preferred_element_type=F32)


def exchanged(value, axis, mask):
    pairs = [(source, source ^ mask) for source in range(lax.axis_size(axis))]
    return lax.ppermute(value, axis, pairs)


def call(body, outs, in_specs, *args, after=(), scratch=(), limit=8, flops=0, nbytes=0):
    count = len(args)

    def ordered(*refs):
        body(*refs[:count], *refs[count + len(after) :])

    return pl.pallas_call(
        ordered if after else body,
        out_shape=outs,
        in_specs=list(in_specs) + [ANY] * len(after),
        out_specs=jax.tree.map(lambda _: VMEM, outs),
        scratch_shapes=list(scratch),
        compiler_params=pltpu.CompilerParams(vmem_limit_bytes=limit * MIB),
        cost_estimate=pl.CostEstimate(flops=flops, bytes_accessed=nbytes, transcendentals=0),
    )(*args, *after)


def shape(dims, dtype):
    return jax.ShapeDtypeStruct(tuple(dims), dtype)


def columns_kernel(order, tail_at, new_at):
    half = lax.axis_index("grp") % 2
    to_row = iota(order.shape, 0)
    wanted = (to_row % ROWS // HALF) * BEAMS + (to_row // ROWS) * HALF + to_row % HALF
    order[...] = (iota(order.shape, 1) == wanted).astype(BF)
    column = iota(tail_at.shape, 0)
    tail_at[...] = (iota(tail_at.shape, 1) == half * HALF + column % HALF).astype(BF)
    column = iota(new_at.shape, 0)
    place = BEAMS + BEAMS * (column // HALF) + half * HALF + column % HALF
    new_at[...] = (iota(new_at.shape, 1) == place).astype(BF)


def slot_rows(source):
    return jnp.concatenate([source[step].astype(F32) for step in range(STEPS)], axis=0)


def feature_part(rows, features):
    me = lax.axis_index("exp")
    mine = rows[:, :features]
    for k in range(1, rows.shape[1] // features):
        mine = jnp.where(me == k, rows[:, k * features : (k + 1) * features], mine)
    return mine


def own_kernel(x_own, wqkv, query, keys, values, part):
    rows = slot_rows(x_own)
    part[...] = feature_part(rows, part.shape[1])
    rows = rows.astype(BF)
    for k, out in enumerate((query, keys, values)):
        out[...] = dot(rows, wqkv[k]).astype(BF)


def in_order(first, own, far):
    return jnp.concatenate([jnp.where(first, own, far), jnp.where(first, far, own)], axis=0)


def pieces(value, count):
    out = []
    for _ in range(count - 1):
        out.append(value.astype(BF).astype(F32))
        value = value - out[-1]
    return out + [value]


def attend_kernel(
    parts,
    order,
    tail_at,
    new_at,
    par_own,
    par_far,
    routes,
    x_far,
    query_own,
    part_own,
    wqkv,
    key_new,
    value_new,
    kp,
    vp,
    tk_raw,
    tv_raw,
    out,
    x_out,
):
    half = lax.axis_index("grp") % 2
    first = half == 0
    width = kp.shape[1]
    heads = width // HDIM
    far_rows = slot_rows(x_far)
    x_out[...] = in_order(first, part_own[...], feature_part(far_rows, part_own.shape[1]))
    query_far = dot(far_rows.astype(BF), wqkv[0]).astype(BF)
    query = in_order(first, query_own[...], query_far)
    lane = iota((BEAMS, LANES), 1)
    beam = iota((BEAMS, LANES), 0)
    state = (lane == beam).astype(F32)
    states = []
    same = iota((HALF, HALF), 0) == iota((HALF, HALF), 1)
    for step in range(STEPS):
        columns = [
            jnp.sum(
                jnp.where(same, source[step : step + 1, :].astype(F32), 0.0),
                axis=1,
                keepdims=True,
            )
            for source in (par_own, par_far)
        ]
        parent = in_order(first, *columns)
        taken = jnp.zeros((BEAMS, LANES), F32)
        for j in range(BEAMS):
            taken = taken + jnp.where(parent == float(j), state[j : j + 1, :], 0.0)
        state = jnp.where(lane == BEAMS + BEAMS * step + beam, 1.0, taken)
        states.append(state)
    held = jnp.concatenate(states, axis=0).astype(BF)
    held = dot(order[...], held).astype(BF)
    held = jnp.concatenate([held] * heads, axis=0)
    spread = jnp.concatenate([query] * heads, axis=0)
    lanes = heads * PAIR
    owner = iota((lanes, width), 0) // PAIR == iota((lanes, width), 1) // HDIM
    spread = jnp.where(owner, spread.astype(F32), 0.0).astype(BF)
    tk = tk_raw[...].reshape(PREV * HALF, width)
    tv = tv_raw[...].reshape(PREV * HALF, width)
    cap = kp.shape[0]
    scale = HDIM ** (-0.5)
    live = iota((cap, lanes), 0) < parts[0]
    s_p = jnp.where(live, dot_t(kp[...], spread) * scale, NEGATIVE)
    s_t = jnp.where(dot_t(tail_at[...], held) > 0.5, dot_t(tk, spread) * scale, NEGATIVE)
    s_n = jnp.where(
        dot_t(new_at[...], held) > 0.5, dot_t(key_new[...], spread) * scale, NEGATIVE
    )
    top = jnp.maximum(
        jnp.max(s_p, axis=0, keepdims=True),
        jnp.maximum(jnp.max(s_t, axis=0, keepdims=True), jnp.max(s_n, axis=0, keepdims=True)),
    )
    p_p, p_t, p_n = [jnp.exp(part - top) for part in (s_p, s_t, s_n)]
    total = (
        jnp.sum(p_p, axis=0, keepdims=True)
        + jnp.sum(p_t, axis=0, keepdims=True)
        + jnp.sum(p_n, axis=0, keepdims=True)
    )
    mix = (
        t_dot(p_p.astype(BF), vp[...])
        + t_dot(p_t.astype(BF), tv)
        + t_dot(p_n.astype(BF), value_new[...])
    )
    columns = jnp.concatenate([top, total, jnp.zeros((6, lanes), F32)], axis=0).T
    info = jnp.zeros((PAIR, LANES), F32)
    info_lane = iota((PAIR, LANES), 1)
    named = slot_rows(routes)
    named = in_order(first, named, jnp.zeros_like(named))
    for k in range(TOPK):
        info = jnp.where(info_lane == 5 * heads + k, named[:, k : k + 1], info)
    for head in range(heads):
        at = slice(head * HDIM, (head + 1) * HDIM)
        these = slice(head * PAIR, (head + 1) * PAIR)
        out[:, at] = mix[these, at].astype(BF)
        parts_of = pieces(columns[these, 0:1], 3) + pieces(columns[these, 1:2], 2)
        for k, column in enumerate(parts_of):
            info = jnp.where(info_lane == k * heads + head, column, info)
    out[:, width:] = info.astype(BF)


def project_kernel(near, far, w_out, *outs):
    me = lax.axis_index("exp")
    width = w_out.shape[0]
    heads = width // HDIM
    parts = []
    infos = [side[:, width:].astype(F32) for side in (near, far)]
    for head in range(heads):
        at = slice(head * HDIM, (head + 1) * HDIM)
        columns = [
            [info[:, k * heads + head : k * heads + head + 1] for k in range(5)] for info in infos
        ]
        (m_near, l_near), (m_far, l_far) = [
            ((c[0] + c[1]) + c[2], c[3] + c[4]) for c in columns
        ]
        top = jnp.maximum(m_near, m_far)
        f_near = jnp.exp(m_near - top)
        f_far = jnp.exp(m_far - top)
        total = l_near * f_near + l_far * f_far
        mix = near[:, at].astype(F32) * f_near + far[:, at].astype(F32) * f_far
        parts.append((mix / total).astype(BF))
    attention = jnp.concatenate(parts, axis=1)
    features = outs[0].shape[1]
    for k, out in enumerate(outs):
        start = pl.multiple_of((me ^ k) * features, LANES)
        out[...] = dot(attention, w_out[:, pl.ds(start, features)]).astype(out.dtype)


def residual_kernel(x, gain, w_router, near, far, own, *rest):
    others, (residual_out, message) = rest[:-2], rest[-2:]
    features = own.shape[1]
    width = near.shape[1] - LANES
    named = near[:, width:].astype(F32) + far[:, width:].astype(F32)
    routes_at = 5 * (width // HDIM)
    residual = x[...] + own[...]
    for other in others:
        residual = residual + other[...].astype(F32)
    residual_out[...] = residual
    rows = (residual * gain[...]).astype(BF)
    message[:, :features] = rows
    logits = dot_t(rows, w_router[...])
    expert = iota(logits.shape, 1).astype(F32)
    lane = iota((PAIR, LANES), 1)
    info = jnp.zeros((PAIR, LANES), F32)
    columns = [jnp.sum(residual * residual, axis=1, keepdims=True)]
    for k in range(TOPK):
        route = named[:, routes_at + k : routes_at + k + 1]
        columns.append(jnp.sum(jnp.where(expert == route, logits, 0.0), axis=1, keepdims=True))
        info = jnp.where(lane == 2 * STATS + k, route, info)
    for at, column in enumerate(columns):
        high = column.astype(BF).astype(F32)
        info = jnp.where(lane == at, high, info)
        info = jnp.where(lane == STATS + at, column - high, info)
    message[:, features:] = info.astype(BF)


def gather_kernel(local, *refs):
    messages, (picked, stats, target, choice, rows) = refs[:-5][::-1], refs[-5:]
    blocks = len(messages)
    tokens = blocks * PAIR
    features = rows.shape[1]
    infos = []
    for k, message in enumerate(messages):
        rows[k * PAIR : (k + 1) * PAIR, :] = message[:, :features]
        infos.append(message[:, features:].astype(F32))
    info = jnp.concatenate(infos, axis=0).T
    stats[...] = jnp.concatenate(
        [info[:STATS] + info[STATS : 2 * STATS], jnp.zeros((8 - STATS, tokens), F32)], axis=0
    )
    first = (lax.axis_index("grp") * local).astype(F32)
    expert = iota((8, tokens), 0).astype(F32)
    chosen = jnp.full((8, tokens), -1.0, F32)
    for k in range(TOPK):
        route = info[2 * STATS + k : 2 * STATS + k + 1] - first
        chosen = jnp.where((route == expert) & (expert < local), float(k), chosen)
    choice[...] = chosen
    named = chosen >= 0.0
    before = iota((tokens, tokens), 0)
    after = iota((tokens, tokens), 1)
    earlier = ((before < after) & (before // ROWS == after // ROWS)).astype(BF)
    rank = dot(named.astype(BF), earlier)
    slot = (iota((8, tokens), 1) // ROWS).astype(F32)
    goal = jnp.where(named, slot * CAP_E + rank, -1.0)
    target[...] = goal
    capacity = picked.shape[1]
    row = iota((capacity, tokens), 0).astype(F32)
    places = [(row == goal[e : e + 1]).astype(F32) for e in range(local)]
    result = dot(jnp.concatenate(places, axis=0).astype(BF), rows[...])
    for e in range(local):
        picked[e] = result[e * capacity : (e + 1) * capacity].astype(BF)


def split_rows(value, rows):
    high = value[:STATS].astype(BF).astype(F32)
    low = value[:STATS] - high
    rest = jnp.zeros((rows - 2 * STATS, value.shape[1]), F32)
    return jnp.concatenate([high, low, rest], axis=0).astype(BF)


def joined_rows(value):
    value = value.astype(F32)
    high, low = value[:STATS], value[STATS : 2 * STATS]
    return jnp.concatenate([high + low, jnp.zeros((8 - STATS, value.shape[1]), F32)], axis=0)


def gate_kernel(places, block, with_stats, count, weights, picked, *refs):
    if with_stats:
        stats, refs = refs[0], refs[1:]
    far, outs = refs[:count], refs[count:]
    me = lax.axis_index("exp")
    width = weights.shape[2]
    for i, (mask, pick) in enumerate(places):
        at = (me ^ mask) * block + pick
        result = dot(picked[at], weights[at])
        if far:
            result = result + far[i][:, :width].astype(F32)
        outs[i][:, :width] = result.astype(outs[i].dtype)
    if with_stats:
        value = stats[...]
        if far:
            value = value + joined_rows(far[0][:, width:])
            outs[-1][...] = value
        outs[0][:, width:] = split_rows(value, outs[0].shape[0])


def gate_block(places, weights, picked, block, stats=(), far=(), dtypes=(BF,), after=(), flops=0):
    capacity, depth = picked.shape[1:]
    width = weights.shape[2]
    outs = [shape((capacity, width), dtype) for dtype in dtypes]
    if stats:
        outs[0] = shape((capacity, width + stats[0].shape[1]), BF)
        if far:
            outs.append(shape(stats[0].shape, F32))
    return call(
        functools.partial(gate_kernel, places, block, bool(stats), len(far)),
        tuple(outs),
        [VMEM] * (2 + len(stats) + len(far)),
        weights,
        picked,
        *stats,
        *far,
        after=after,
        flops=flops,
    )


def place_kernel(local, target, choice, stats, far, high, low):
    stats = stats[...] + joined_rows(far[:, far.shape[1] - target.shape[1] :])
    inverse = lax.rsqrt(stats[0:1] / MODEL + EPSILON)
    logits = [stats[1 + k : 2 + k] * inverse for k in range(TOPK)]
    top = functools.reduce(jnp.maximum, logits)
    weights = [jnp.exp(logit - top) for logit in logits]
    whole = functools.reduce(lambda a, b: a + b, weights)
    chosen = choice[...]
    share = jnp.zeros(chosen.shape, F32)
    for k in range(TOPK):
        share = jnp.where(chosen == float(k), weights[k] / whole, share)
    row = iota(high.shape[1:], 0).astype(F32)
    for e in range(local):
        place = jnp.where(row == target[e : e + 1, :], share[e : e + 1], 0.0)
        rounded = place.astype(BF)
        high[e] = rounded
        low[e] = (place - rounded.astype(F32)).astype(BF)


def hidden_kernel(block, pick, near, mid, far, target, stats, far_stats, hidden):
    capacity = near.shape[0]
    stats = stats[...] + joined_rows(far_stats[:, far_stats.shape[1] - target.shape[1] :])
    inverse = lax.rsqrt(stats[0:1] / MODEL + EPSILON)
    goal = target[pl.ds(lax.axis_index("exp") * block + pick, 1), :]
    row = iota((capacity, target.shape[1]), 0).astype(F32)
    scale = jnp.sum(jnp.where(row == goal, inverse, 0.0), axis=1, keepdims=True)
    half = near.shape[1] // 2
    gate = near[:, :half] + mid[:, :half].astype(F32) + far[:, :half].astype(F32)
    up = near[:, half:] + mid[:, half:].astype(F32) + far[:, half : 2 * half].astype(F32)
    gate, up = gate * scale, up * scale
    hidden[...] = (gate / (1.0 + jnp.exp(-gate)) * up).astype(BF)


def down_kernel(places, block, last, count, weights, high, low, *refs):
    hiddens, refs = refs[: len(places)], refs[len(places) :]
    before, refs = refs[:count], refs[count:]
    me = lax.axis_index("exp")
    mixed = before[0][...] if before else 0.0
    for hidden, (mask, pick) in zip(hiddens, places):
        at = (me ^ mask) * block + pick
        result = dot_t(hidden[...], weights[at]).astype(BF)
        mixed = mixed + (t_dot(high[at], result) + t_dot(low[at], result))
    if not last:
        refs[0][...] = mixed
        return
    send, rows = refs
    rows[...] = mixed
    request = lax.axis_index("grp") // 2
    for group in range(send.shape[0]):
        start = ((group // 2) ^ request) * PAIR + group % 2 * ROWS
        send[group] = rows[pl.ds(pl.multiple_of(start, ROWS), ROWS), :].astype(BF)


def down_blocks(places, hiddens, weights, high, low, block, before=(), last=False, after=()):
    features, width = weights.shape[1:]
    tokens = high.shape[2]
    if last:
        out = shape((tokens // ROWS, ROWS, features), BF)
    else:
        out = shape((tokens, features), F32)
    return call(
        functools.partial(down_kernel, places, block, last, len(before)),
        out,
        [VMEM] * (3 + len(hiddens) + len(before)),
        weights,
        high,
        low,
        *hiddens,
        *before,
        after=after,
        scratch=[pltpu.VMEM((tokens, features), F32)] if last else [],
    )


def finish_kernel(residual, back, out):
    half = lax.axis_index("grp") % 2
    value = residual[pl.ds(pl.multiple_of(half * ROWS, ROWS), ROWS), :]
    for group in range(back.shape[0]):
        value = value + back[group].astype(F32)
    out[...] = value.astype(out.dtype)


def on_device(
    step_inputs,
    parents,
    routes,
    w_qkv,
    w_out,
    prompt_keys,
    prompt_values,
    prompt_parts,
    tail_keys,
    tail_values,
    w_router,
    norm_gain,
    w_gate_up,
    w_down,
):
    groups = lax.axis_size("grp")
    splits = lax.axis_size("exp")
    requests = groups // 2
    model = w_qkv.shape[0]
    width = w_qkv.shape[2]
    features = norm_gain.shape[0]
    local = w_gate_up.shape[0]
    tokens = requests * PAIR

    w_all = w_qkv.transpose(1, 0, 2)
    columns = call(
        columns_kernel,
        (
            shape((PAIR, PAIR), BF),
            shape((PREV * HALF, LANES), BF),
            shape((ROWS, LANES), BF),
        ),
        [],
        flops=HINT,
    )
    own_inputs, own_parents, columns = lax.optimization_barrier(
        (step_inputs[0], parents[0], columns)
    )
    far_inputs, far_parents = exchanged((own_inputs, own_parents), "grp", 1)
    query, keys_new, values_new, part = call(
        own_kernel,
        (shape((ROWS, width), BF),) * 3 + (shape((ROWS, features), F32),),
        [VMEM] * 2,
        step_inputs[0],
        w_all,
        after=columns[:1],
        flops=HINT // 4,
    )
    near, x = call(
        attend_kernel,
        (shape((PAIR, width + LANES), BF), shape((PAIR, features), F32)),
        [SMEM] + [VMEM] * 16,
        prompt_parts,
        *columns,
        parents[0],
        far_parents,
        routes[0],
        far_inputs,
        query,
        part,
        w_all,
        keys_new,
        values_new,
        prompt_keys[0],
        prompt_values[0],
        tail_keys[0].transpose(1, 0, 2),
        tail_values[0].transpose(1, 0, 2),
        flops=HINT,
    )
    far = exchanged(near, "grp", 1)
    terms = call(
        project_kernel,
        tuple(shape((PAIR, features), F32 if k == 0 else BF) for k in range(splits)),
        [VMEM] * 3,
        near,
        far,
        w_out,
        flops=HINT,
    )
    arrived = [exchanged(terms[k], "exp", k) for k in range(1, splits)]
    residual, message = call(
        residual_kernel,
        (shape((PAIR, features), F32), shape((PAIR, features + LANES), BF)),
        [VMEM] * (6 + len(arrived)),
        x,
        norm_gain.reshape(1, features),
        w_router.T,
        near,
        far,
        terms[0],
        *arrived,
        flops=HINT,
    )
    messages = [exchanged(message, "grp", 2 * k) for k in range(1, requests)]
    messages = [message] + messages
    picked, stats, target, choice = call(
        functools.partial(gather_kernel, local),
        (
            shape((local, EXPERTS * CAP_E // local, features), BF),
            shape((8, tokens), F32),
            shape((8, tokens), F32),
            shape((8, tokens), F32),
        ),
        [VMEM] * requests,
        *messages[::-1],
        scratch=[pltpu.VMEM((tokens, features), BF)],
        flops=HINT,
    )
    if splits == 4 and local == 2 * splits:
        gate = functools.partial(gate_block, weights=w_gate_up, picked=picked, block=2)
        (a0,) = gate(((3, 0),), stats=(stats,))
        far_a0 = exchanged(a0, "exp", 1)
        (a1,) = gate(((3, 1),), after=(a0,))
        far_a1 = exchanged(a1, "exp", 1)
        c0, stats = gate(((2, 0),), stats=(stats,), far=(far_a0,), after=(a1,))
        far_c0 = exchanged(c0, "exp", 2)
        (c1,) = gate(((2, 1),), far=(far_a1,), after=(c0,))
        far_c1 = exchanged(c1, "exp", 2)
        b0, b1, d0, d1 = gate(
            ((1, 0), (1, 1), (0, 0), (0, 1)),
            dtypes=(BF, BF, F32, F32),
            after=(c1,),
            flops=5000000000,
        )
        far_b0, far_b1 = exchanged((b0, b1), "exp", 1)

        def hidden_of(pick, near, mid, far, after=()):
            return call(
                functools.partial(hidden_kernel, 2, pick),
                shape((near.shape[0], FFE), BF),
                [VMEM] * 6,
                near,
                mid,
                far,
                target,
                stats,
                far_c0,
                after=after,
                flops=2000000000,
            )

        own0 = hidden_of(0, d0, far_b0, far_c0)
        core0 = exchanged(own0, "exp", 1)
        y0 = exchanged(own0, "exp", 2)
        place = shape((local, picked.shape[1], tokens), BF)
        high, low = call(
            functools.partial(place_kernel, local),
            (place, place),
            [VMEM] * 4,
            target,
            choice,
            stats,
            far_c0,
            after=(own0,),
            flops=2000000000,
        )
        down = functools.partial(down_blocks, weights=w_down, high=high, low=low, block=2)
        mixed = down(((0, 0), (1, 0)), (own0, core0))
        own1 = hidden_of(1, d1, far_b1, far_c1, after=(mixed,))
        core1 = exchanged(own1, "exp", 1)
        y1 = exchanged(own1, "exp", 2)
        mixed = down(((0, 1), (1, 1)), (own1, core1), before=(mixed,))
        far0 = exchanged(y0, "exp", 1)
        mixed = down(((2, 0),), (y0,), before=(mixed,))
        y1, mixed = lax.optimization_barrier((y1, mixed))
        far1 = exchanged(y1, "exp", 1)
        mixed = down(((2, 1), (3, 0)), (y1, far0), before=(mixed,))
        send = down(((3, 1),), (far1,), before=(mixed,), last=True)
    else:
        stats = lax.psum(stats, "exp")
        sums = jnp.einsum("lcd,ldf->lcf", picked, w_gate_up, preferred_element_type=F32)
        sums = lax.psum(sums.astype(BF), "exp").astype(F32)
        inverse = lax.rsqrt(stats[0] / model + EPSILON)
        goal, pick = target[:local], choice[:local]
        place = goal[:, None, :] == jnp.arange(picked.shape[1], dtype=F32)[None, :, None]
        sums = sums * jnp.sum(jnp.where(place, inverse, 0.0), axis=2, keepdims=True)
        hidden = (jax.nn.silu(sums[..., :FFE]) * sums[..., FFE:]).astype(BF)
        result = jnp.einsum("lcf,ldf->lcd", hidden, w_down, preferred_element_type=F32)
        share = jax.nn.softmax(stats[1:STATS] * inverse, axis=0)
        ids = jnp.arange(TOPK, dtype=F32)[None, :, None]
        weight = jnp.sum(jnp.where(pick[:, None, :] == ids, share[None], 0.0), axis=1)
        mixed = jnp.einsum(
            "lct,lcd->td",
            jnp.where(place, weight[:, None, :], 0.0),
            result.astype(BF).astype(F32),
            precision=lax.Precision.HIGHEST,
        ).reshape(requests, 2 * ROWS, features)
        order = jnp.arange(requests) ^ (lax.axis_index("grp") // 2)
        send = mixed[order].reshape(groups, ROWS, features).astype(BF)
    back = lax.all_to_all(send, "grp", split_axis=0, concat_axis=0, tiled=True)
    result = call(
        finish_kernel, shape((ROWS, features), BF), [VMEM] * 2, residual, back
    )
    return result.reshape(1, STEPS, HALF, features)


def solution(mesh):
    placed = (
        P("grp", None, None, None),
        P("grp", None, None),
        P("grp", None, None, None),
        P(None, None, "exp"),
        P("exp", None),
        P("grp", None, "exp"),
        P("grp", None, "exp"),
        P("grp"),
        P("grp", None, None, "exp"),
        P("grp", None, None, "exp"),
        P("exp", None),
        P("exp"),
        P("grp", "exp", None),
        P("grp", "exp", None),
    )
    return jax.shard_map(
        on_device,
        mesh=mesh,
        in_specs=placed,
        out_specs=P("grp", None, None, "exp"),
        check_vma=False,
    )
```

```python
import functools

import jax
import jax.numpy as jnp
from jax import lax
from jax.experimental import pallas as pl
from jax.experimental.pallas import tpu as pltpu
from jax.sharding import PartitionSpec as P

HDIM = 128
EXPERTS = 64
FFE = 1408
TOPK = 6
BEAMS = 8
STEPS = 4
CAP_E = 3
HALF = 4
PREV = 60
LANES = 128
MODEL = 2048
ROWS = STEPS * HALF
PAIR = 2 * ROWS
STATS = 1 + TOPK

NEGATIVE = -1e30
EPSILON = 1e-06
MIB = 1024 * 1024
BF = jnp.bfloat16
HINT = 10**10
F32 = jnp.float32

VMEM = pl.BlockSpec(memory_space=pltpu.VMEM)
SMEM = pl.BlockSpec(memory_space=pltpu.SMEM)
ANY = pl.BlockSpec(memory_space=pl.ANY)


def iota(shape, dim):
    return lax.broadcasted_iota(jnp.int32, shape, dim)


def dot(a, b):
    return jnp.dot(a, b, preferred_element_type=F32)


def dot_t(a, b):
    return lax.dot_general(a, b, (((1,), (1,)), ((), ())), preferred_element_type=F32)


def t_dot(a, b):
    return lax.dot_general(a, b, (((0,), (0,)), ((), ())), preferred_element_type=F32)


def exchanged(value, axis, mask):
    pairs = [(source, source ^ mask) for source in range(lax.axis_size(axis))]
    return lax.ppermute(value, axis, pairs)


def call(body, outs, in_specs, *args, after=(), scratch=(), limit=8, flops=0, nbytes=0):
    count = len(args)

    def ordered(*refs):
        body(*refs[:count], *refs[count + len(after) :])

    return pl.pallas_call(
        ordered if after else body,
        out_shape=outs,
        in_specs=list(in_specs) + [ANY] * len(after),
        out_specs=jax.tree.map(lambda _: VMEM, outs),
        scratch_shapes=list(scratch),
        compiler_params=pltpu.CompilerParams(vmem_limit_bytes=limit * MIB),
        cost_estimate=pl.CostEstimate(flops=flops, bytes_accessed=nbytes, transcendentals=0),
    )(*args, *after)


def shape(dims, dtype):
    return jax.ShapeDtypeStruct(tuple(dims), dtype)


def columns_kernel(order, tail_at, new_at):
    half = lax.axis_index("grp") % 2
    to_row = iota(order.shape, 0)
    wanted = (to_row % ROWS // HALF) * BEAMS + (to_row // ROWS) * HALF + to_row % HALF
    order[...] = (iota(order.shape, 1) == wanted).astype(BF)
    column = iota(tail_at.shape, 0)
    tail_at[...] = (iota(tail_at.shape, 1) == half * HALF + column % HALF).astype(BF)
    column = iota(new_at.shape, 0)
    place = BEAMS + BEAMS * (column // HALF) + half * HALF + column % HALF
    new_at[...] = (iota(new_at.shape, 1) == place).astype(BF)


def slot_rows(source):
    return jnp.concatenate([source[step].astype(F32) for step in range(STEPS)], axis=0)


def feature_part(rows, features):
    me = lax.axis_index("exp")
    mine = rows[:, :features]
    for k in range(1, rows.shape[1] // features):
        mine = jnp.where(me == k, rows[:, k * features : (k + 1) * features], mine)
    return mine


def send_kernel(x_own, parents, routes, out):
    rows = slot_rows(x_own)
    depth = rows.shape[1]
    out[:, :depth] = rows.astype(BF)
    lane = iota((ROWS, LANES), 1)
    info = jnp.zeros((ROWS, LANES), F32)
    named = slot_rows(routes)
    for k in range(TOPK):
        info = jnp.where(lane == k, named[:, k : k + 1], info)
    same = iota((HALF, HALF), 0) == iota((HALF, HALF), 1)
    columns = [
        jnp.sum(
            jnp.where(same, parents[step : step + 1, :].astype(F32), 0.0), axis=1, keepdims=True
        )
        for step in range(STEPS)
    ]
    info = jnp.where(lane == TOPK, jnp.concatenate(columns, axis=0), info)
    out[:, depth:] = info.astype(BF)


def own_kernel(sent, wqkv, tk_raw, tv_raw, query, keys, values, part, tk, tv):
    rows = sent[:, : wqkv.shape[1]]
    part[...] = feature_part(rows.astype(F32), part.shape[1])
    for k, out in enumerate((query, keys, values)):
        out[...] = dot(rows, wqkv[k]).astype(BF)
    tk[...] = tk_raw[...].reshape(tk.shape)
    tv[...] = tv_raw[...].reshape(tv.shape)


def in_order(first, own, far):
    return jnp.concatenate([jnp.where(first, own, far), jnp.where(first, far, own)], axis=0)


def pieces(value, count):
    out = []
    for _ in range(count - 1):
        out.append(value.astype(BF).astype(F32))
        value = value - out[-1]
    return out + [value]


def attend_kernel(
    parts,
    order,
    tail_at,
    new_at,
    sent,
    came,
    query_own,
    part_own,
    wqkv,
    key_new,
    value_new,
    kp,
    vp,
    tk,
    tv,
    out,
    x_out,
    named,
):
    half = lax.axis_index("grp") % 2
    first = half == 0
    width = kp.shape[1]
    heads = width // HDIM
    depth = wqkv.shape[1]
    far_rows = came[:, :depth]
    part_far = feature_part(far_rows.astype(F32), part_own.shape[1])
    x_out[...] = in_order(first, part_own[...], part_far)
    names = in_order(first, sent[:, depth:].astype(F32), came[:, depth:].astype(F32))
    named[...] = names
    parents = names[:, TOPK : TOPK + 1]
    query_far = dot(far_rows, wqkv[0]).astype(BF)
    query = in_order(first, query_own[...], query_far)
    lane = iota((BEAMS, LANES), 1)
    beam = iota((BEAMS, LANES), 0)
    state = (lane == beam).astype(F32)
    states = []
    for step in range(STEPS):
        at = step * HALF
        parent = jnp.concatenate(
            [parents[at : at + HALF], parents[ROWS + at : ROWS + at + HALF]], axis=0
        )
        taken = jnp.zeros((BEAMS, LANES), F32)
        for j in range(BEAMS):
            taken = taken + jnp.where(parent == float(j), state[j : j + 1, :], 0.0)
        state = jnp.where(lane == BEAMS + BEAMS * step + beam, 1.0, taken)
        states.append(state)
    held = jnp.concatenate(states, axis=0).astype(BF)
    held = dot(order[...], held).astype(BF)
    held = jnp.concatenate([held] * heads, axis=0)
    spread = jnp.concatenate([query] * heads, axis=0)
    lanes = heads * PAIR
    owner = iota((lanes, width), 0) // PAIR == iota((lanes, width), 1) // HDIM
    spread = jnp.where(owner, spread.astype(F32), 0.0).astype(BF)
    cap = kp.shape[0]
    scale = HDIM ** (-0.5)
    live = iota((cap, lanes), 0) < parts[0]
    s_p = jnp.where(live, dot_t(kp[...], spread) * scale, NEGATIVE)
    s_t = jnp.where(dot_t(tail_at[...], held) > 0.5, dot_t(tk[...], spread) * scale, NEGATIVE)
    s_n = jnp.where(
        dot_t(new_at[...], held) > 0.5, dot_t(key_new[...], spread) * scale, NEGATIVE
    )
    top = jnp.maximum(
        jnp.max(s_p, axis=0, keepdims=True),
        jnp.maximum(jnp.max(s_t, axis=0, keepdims=True), jnp.max(s_n, axis=0, keepdims=True)),
    )
    p_p, p_t, p_n = [jnp.exp(part - top) for part in (s_p, s_t, s_n)]
    total = (
        jnp.sum(p_p, axis=0, keepdims=True)
        + jnp.sum(p_t, axis=0, keepdims=True)
        + jnp.sum(p_n, axis=0, keepdims=True)
    )
    mix = (
        t_dot(p_p.astype(BF), vp[...])
        + t_dot(p_t.astype(BF), tv[...])
        + t_dot(p_n.astype(BF), value_new[...])
    )
    columns = jnp.concatenate([top, total, jnp.zeros((6, lanes), F32)], axis=0).T
    info = jnp.zeros((PAIR, LANES), F32)
    info_lane = iota((PAIR, LANES), 1)
    for head in range(heads):
        at = slice(head * HDIM, (head + 1) * HDIM)
        these = slice(head * PAIR, (head + 1) * PAIR)
        out[:, at] = mix[these, at].astype(BF)
        parts_of = pieces(columns[these, 0:1], 3) + pieces(columns[these, 1:2], 2)
        for k, column in enumerate(parts_of):
            info = jnp.where(info_lane == k * heads + head, column, info)
    out[:, width:] = info.astype(BF)


def project_kernel(near, far, w_out, *outs):
    me = lax.axis_index("exp")
    width = w_out.shape[0]
    heads = width // HDIM
    parts = []
    infos = [side[:, width:].astype(F32) for side in (near, far)]
    for head in range(heads):
        at = slice(head * HDIM, (head + 1) * HDIM)
        columns = [
            [info[:, k * heads + head : k * heads + head + 1] for k in range(5)] for info in infos
        ]
        (m_near, l_near), (m_far, l_far) = [
            ((c[0] + c[1]) + c[2], c[3] + c[4]) for c in columns
        ]
        top = jnp.maximum(m_near, m_far)
        f_near = jnp.exp(m_near - top)
        f_far = jnp.exp(m_far - top)
        total = l_near * f_near + l_far * f_far
        mix = near[:, at].astype(F32) * f_near + far[:, at].astype(F32) * f_far
        parts.append((mix / total).astype(BF))
    attention = jnp.concatenate(parts, axis=1)
    features = outs[0].shape[1]
    for k, out in enumerate(outs):
        start = pl.multiple_of((me ^ k) * features, LANES)
        out[...] = dot(attention, w_out[:, pl.ds(start, features)]).astype(out.dtype)


def residual_kernel(x, named, gain, w_router, own, *rest):
    others, (residual_out, message) = rest[:-2], rest[-2:]
    features = own.shape[1]
    residual = x[...] + own[...]
    for other in others:
        residual = residual + other[...].astype(F32)
    residual_out[...] = residual
    rows = (residual * gain[...]).astype(BF)
    message[:, :features] = rows
    logits = dot_t(rows, w_router[...])
    expert = iota(logits.shape, 1).astype(F32)
    lane = iota((PAIR, LANES), 1)
    info = jnp.zeros((PAIR, LANES), F32)
    columns = [jnp.sum(residual * residual, axis=1, keepdims=True)]
    for k in range(TOPK):
        route = named[:, k : k + 1]
        columns.append(jnp.sum(jnp.where(expert == route, logits, 0.0), axis=1, keepdims=True))
        info = jnp.where(lane == 2 * STATS + k, route, info)
    for at, column in enumerate(columns):
        high = column.astype(BF).astype(F32)
        info = jnp.where(lane == at, high, info)
        info = jnp.where(lane == STATS + at, column - high, info)
    message[:, features:] = info.astype(BF)


def gather_kernel(local, *refs):
    messages, (picked, stats, target, choice, rows, infos) = refs[:-6], refs[-6:]
    blocks = len(messages)
    tokens = blocks * PAIR
    features = rows.shape[1]
    request = lax.axis_index("grp") // 2
    for k, message in enumerate(messages):
        at = pl.ds(pl.multiple_of((request ^ k) * PAIR, PAIR), PAIR)
        rows[at, :] = message[:, :features]
        infos[at, :] = message[:, features:].astype(F32)
    info = infos[...].T
    stats[...] = jnp.concatenate(
        [info[:STATS] + info[STATS : 2 * STATS], jnp.zeros((8 - STATS, tokens), F32)], axis=0
    )
    first = (lax.axis_index("grp") * local).astype(F32)
    expert = iota((8, tokens), 0).astype(F32)
    chosen = jnp.full((8, tokens), -1.0, F32)
    for k in range(TOPK):
        route = info[2 * STATS + k : 2 * STATS + k + 1] - first
        chosen = jnp.where((route == expert) & (expert < local), float(k), chosen)
    choice[...] = chosen
    named = chosen >= 0.0
    before = iota((tokens, tokens), 0)
    after = iota((tokens, tokens), 1)
    earlier = ((before < after) & (before // ROWS == after // ROWS)).astype(BF)
    rank = dot(named.astype(BF), earlier)
    slot = (iota((8, tokens), 1) // ROWS).astype(F32)
    goal = jnp.where(named, slot * CAP_E + rank, -1.0)
    target[...] = goal
    capacity = picked.shape[1]
    row = iota((capacity, tokens), 0).astype(F32)
    places = [(row == goal[e : e + 1]).astype(F32) for e in range(local)]
    result = dot(jnp.concatenate(places, axis=0).astype(BF), rows[...])
    for e in range(local):
        picked[e] = result[e * capacity : (e + 1) * capacity].astype(BF)


def split_rows(value, rows):
    high = value[:STATS].astype(BF).astype(F32)
    low = value[:STATS] - high
    rest = jnp.zeros((rows - 2 * STATS, value.shape[1]), F32)
    return jnp.concatenate([high, low, rest], axis=0).astype(BF)


def joined_rows(value):
    value = value.astype(F32)
    high, low = value[:STATS], value[STATS : 2 * STATS]
    return jnp.concatenate([high + low, jnp.zeros((8 - STATS, value.shape[1]), F32)], axis=0)


def gate_kernel(places, block, with_stats, count, weights, picked, *refs):
    if with_stats:
        stats, refs = refs[0], refs[1:]
    far, outs = refs[:count], refs[count:]
    me = lax.axis_index("exp")
    width = weights.shape[2]
    for i, (mask, pick) in enumerate(places):
        at = (me ^ mask) * block + pick
        result = dot(picked[at], weights[at])
        if far:
            result = result + far[i][:, :width].astype(F32)
        outs[i][:, :width] = result.astype(outs[i].dtype)
    if with_stats:
        value = stats[...]
        if far:
            value = value + joined_rows(far[0][:, width:])
            outs[-1][...] = value
        outs[0][:, width:] = split_rows(value, outs[0].shape[0])


def gate_block(places, weights, picked, block, stats=(), far=(), dtypes=(BF,), after=(), flops=0):
    capacity, depth = picked.shape[1:]
    width = weights.shape[2]
    outs = [shape((capacity, width), dtype) for dtype in dtypes]
    if stats:
        outs[0] = shape((capacity, width + stats[0].shape[1]), BF)
        if far:
            outs.append(shape(stats[0].shape, F32))
    return call(
        functools.partial(gate_kernel, places, block, bool(stats), len(far)),
        tuple(outs),
        [VMEM] * (2 + len(stats) + len(far)),
        weights,
        picked,
        *stats,
        *far,
        after=after,
        flops=flops,
    )


def place_kernel(local, target, choice, stats, far, high, low):
    stats = stats[...] + joined_rows(far[:, far.shape[1] - target.shape[1] :])
    inverse = lax.rsqrt(stats[0:1] / MODEL + EPSILON)
    logits = [stats[1 + k : 2 + k] * inverse for k in range(TOPK)]
    top = functools.reduce(jnp.maximum, logits)
    weights = [jnp.exp(logit - top) for logit in logits]
    whole = functools.reduce(lambda a, b: a + b, weights)
    chosen = choice[...]
    share = jnp.zeros(chosen.shape, F32)
    for k in range(TOPK):
        share = jnp.where(chosen == float(k), weights[k] / whole, share)
    row = iota(high.shape[1:], 0).astype(F32)
    for e in range(local):
        place = jnp.where(row == target[e : e + 1, :], share[e : e + 1], 0.0)
        rounded = place.astype(BF)
        high[e] = rounded
        low[e] = (place - rounded.astype(F32)).astype(BF)


def hidden_kernel(block, pick, near, mid, far, target, stats, far_stats, hidden):
    capacity = near.shape[0]
    stats = stats[...] + joined_rows(far_stats[:, far_stats.shape[1] - target.shape[1] :])
    inverse = lax.rsqrt(stats[0:1] / MODEL + EPSILON)
    goal = target[pl.ds(lax.axis_index("exp") * block + pick, 1), :]
    row = iota((capacity, target.shape[1]), 0).astype(F32)
    scale = jnp.sum(jnp.where(row == goal, inverse, 0.0), axis=1, keepdims=True)
    half = near.shape[1] // 2
    gate = near[:, :half] + mid[:, :half].astype(F32) + far[:, :half].astype(F32)
    up = near[:, half:] + mid[:, half:].astype(F32) + far[:, half : 2 * half].astype(F32)
    gate, up = gate * scale, up * scale
    hidden[...] = (gate / (1.0 + jnp.exp(-gate)) * up).astype(BF)


def down_kernel(places, block, last, count, weights, high, low, *refs):
    hiddens, refs = refs[: len(places)], refs[len(places) :]
    before, refs = refs[:count], refs[count:]
    me = lax.axis_index("exp")
    mixed = before[0][...] if before else 0.0
    for hidden, (mask, pick) in zip(hiddens, places):
        at = (me ^ mask) * block + pick
        result = dot_t(hidden[...], weights[at]).astype(BF)
        mixed = mixed + (t_dot(high[at], result) + t_dot(low[at], result))
    if not last:
        refs[0][...] = mixed
        return
    refs[0][...] = mixed.astype(BF).reshape(refs[0].shape)


def down_blocks(places, hiddens, weights, high, low, block, before=(), last=False, after=()):
    features, width = weights.shape[1:]
    tokens = high.shape[2]
    if last:
        out = shape((tokens // ROWS, ROWS, features), BF)
    else:
        out = shape((tokens, features), F32)
    return call(
        functools.partial(down_kernel, places, block, last, len(before)),
        out,
        [VMEM] * (3 + len(hiddens) + len(before)),
        weights,
        high,
        low,
        *hiddens,
        *before,
        after=after,
    )


def finish_kernel(residual, back, out):
    half = lax.axis_index("grp") % 2
    value = residual[pl.ds(pl.multiple_of(half * ROWS, ROWS), ROWS), :]
    for group in range(back.shape[0]):
        value = value + back[group].astype(F32)
    out[...] = value.astype(out.dtype)


def on_device(
    step_inputs,
    parents,
    routes,
    w_qkv,
    w_out,
    prompt_keys,
    prompt_values,
    prompt_parts,
    tail_keys,
    tail_values,
    w_router,
    norm_gain,
    w_gate_up,
    w_down,
):
    groups = lax.axis_size("grp")
    splits = lax.axis_size("exp")
    requests = groups // 2
    model = w_qkv.shape[0]
    width = w_qkv.shape[2]
    features = norm_gain.shape[0]
    local = w_gate_up.shape[0]
    tokens = requests * PAIR

    w_all = w_qkv.transpose(1, 0, 2)
    columns = call(
        columns_kernel,
        (
            shape((PAIR, PAIR), BF),
            shape((PREV * HALF, LANES), BF),
            shape((ROWS, LANES), BF),
        ),
        [],
        flops=HINT,
    )
    sent = call(
        send_kernel,
        shape((ROWS, model + LANES), BF),
        [VMEM] * 3,
        step_inputs[0],
        parents[0],
        routes[0],
        after=columns[:1],
    )
    came = exchanged(sent, "grp", 1)
    query, keys_new, values_new, part, tail_k, tail_v = call(
        own_kernel,
        (shape((ROWS, width), BF),) * 3
        + (shape((ROWS, features), F32),)
        + (shape((PREV * HALF, width), BF),) * 2,
        [VMEM] * 4,
        sent,
        w_all,
        tail_keys[0].transpose(1, 0, 2),
        tail_values[0].transpose(1, 0, 2),
        flops=HINT // 4,
    )
    near, x, named = call(
        attend_kernel,
        (
            shape((PAIR, width + LANES), BF),
            shape((PAIR, features), F32),
            shape((PAIR, LANES), F32),
        ),
        [SMEM] + [VMEM] * 14,
        prompt_parts,
        *columns,
        sent,
        came,
        query,
        part,
        w_all,
        keys_new,
        values_new,
        prompt_keys[0],
        prompt_values[0],
        tail_k,
        tail_v,
        flops=HINT,
    )
    far = exchanged(near, "grp", 1)
    terms = call(
        project_kernel,
        tuple(shape((PAIR, features), F32 if k == 0 else BF) for k in range(splits)),
        [VMEM] * 3,
        near,
        far,
        w_out,
        flops=HINT,
    )
    arrived = [exchanged(terms[k], "exp", k) for k in range(1, splits)]
    residual, message = call(
        residual_kernel,
        (shape((PAIR, features), F32), shape((PAIR, features + LANES), BF)),
        [VMEM] * (5 + len(arrived)),
        x,
        named,
        norm_gain.reshape(1, features),
        w_router.T,
        terms[0],
        *arrived,
        flops=HINT,
    )
    messages = [exchanged(message, "grp", 2 * k) for k in range(1, requests)]
    messages = [message] + messages
    picked, stats, target, choice = call(
        functools.partial(gather_kernel, local),
        (
            shape((local, EXPERTS * CAP_E // local, features), BF),
            shape((8, tokens), F32),
            shape((8, tokens), F32),
            shape((8, tokens), F32),
        ),
        [VMEM] * requests,
        *messages,
        scratch=[pltpu.VMEM((tokens, features), BF), pltpu.VMEM((tokens, LANES), F32)],
        flops=HINT,
    )
    if splits == 4 and local == 2 * splits:
        gate = functools.partial(gate_block, weights=w_gate_up, picked=picked, block=2)
        (a0,) = gate(((3, 0),), stats=(stats,))
        far_a0 = exchanged(a0, "exp", 1)
        (a1,) = gate(((3, 1),), after=(a0,))
        far_a1 = exchanged(a1, "exp", 1)
        c0, stats = gate(((2, 0),), stats=(stats,), far=(far_a0,), after=(a1,))
        far_c0 = exchanged(c0, "exp", 2)
        (c1,) = gate(((2, 1),), far=(far_a1,), after=(c0,))
        far_c1 = exchanged(c1, "exp", 2)
        b0, d0 = gate(((1, 0), (0, 0)), dtypes=(BF, F32), after=(c1,), flops=30 * HINT // 100)
        far_b0 = exchanged(b0, "exp", 1)
        b1, d1 = gate(((1, 1), (0, 1)), dtypes=(BF, F32), after=(d0,), flops=30 * HINT // 100)
        far_b1 = exchanged(b1, "exp", 1)

        def hidden_of(pick, near, mid, far, after=()):
            return call(
                functools.partial(hidden_kernel, 2, pick),
                shape((near.shape[0], FFE), BF),
                [VMEM] * 6,
                near,
                mid,
                far,
                target,
                stats,
                far_c0,
                after=after,
                flops=10 * HINT // 100,
            )

        own0 = hidden_of(0, d0, far_b0, far_c0, after=(d1,))
        core0 = exchanged(own0, "exp", 1)
        y0 = exchanged(own0, "exp", 2)
        place = shape((local, picked.shape[1], tokens), BF)
        high, low = call(
            functools.partial(place_kernel, local),
            (place, place),
            [VMEM] * 4,
            target,
            choice,
            stats,
            far_c0,
            after=(own0,),
            flops=10 * HINT // 100,
        )
        down = functools.partial(down_blocks, weights=w_down, high=high, low=low, block=2)
        own1 = hidden_of(1, d1, far_b1, far_c1, after=(high,))
        core1 = exchanged(own1, "exp", 1)
        y1 = exchanged(own1, "exp", 2)
        mixed = down(((0, 0), (1, 0)), (own0, core0), after=(own1,))
        y0, mixed = lax.optimization_barrier((y0, mixed))
        far0 = exchanged(y0, "exp", 1)
        mixed = down(((0, 1), (1, 1), (2, 0)), (own1, core1, y0), before=(mixed,))
        y1, mixed = lax.optimization_barrier((y1, mixed))
        far1 = exchanged(y1, "exp", 1)
        mixed = down(((3, 0), (2, 1)), (far0, y1), before=(mixed,))
        send = down(((3, 1),), (far1,), before=(mixed,), last=True)
    else:
        stats = lax.psum(stats, "exp")
        sums = jnp.einsum("lcd,ldf->lcf", picked, w_gate_up, preferred_element_type=F32)
        sums = lax.psum(sums.astype(BF), "exp").astype(F32)
        inverse = lax.rsqrt(stats[0] / model + EPSILON)
        goal, pick = target[:local], choice[:local]
        place = goal[:, None, :] == jnp.arange(picked.shape[1], dtype=F32)[None, :, None]
        sums = sums * jnp.sum(jnp.where(place, inverse, 0.0), axis=2, keepdims=True)
        hidden = (jax.nn.silu(sums[..., :FFE]) * sums[..., FFE:]).astype(BF)
        result = jnp.einsum("lcf,ldf->lcd", hidden, w_down, preferred_element_type=F32)
        share = jax.nn.softmax(stats[1:STATS] * inverse, axis=0)
        ids = jnp.arange(TOPK, dtype=F32)[None, :, None]
        weight = jnp.sum(jnp.where(pick[:, None, :] == ids, share[None], 0.0), axis=1)
        mixed = jnp.einsum(
            "lct,lcd->td",
            jnp.where(place, weight[:, None, :], 0.0),
            result.astype(BF).astype(F32),
            precision=lax.Precision.HIGHEST,
        )
        send = mixed.reshape(groups, ROWS, features).astype(BF)
    back = lax.all_to_all(send, "grp", split_axis=0, concat_axis=0, tiled=True)
    result = call(
        finish_kernel, shape((ROWS, features), BF), [VMEM] * 2, residual, back
    )
    return result.reshape(1, STEPS, HALF, features)


def solution(mesh):
    placed = (
        P("grp", None, None, None),
        P("grp", None, None),
        P("grp", None, None, None),
        P(None, None, "exp"),
        P("exp", None),
        P("grp", None, "exp"),
        P("grp", None, "exp"),
        P("grp"),
        P("grp", None, None, "exp"),
        P("grp", None, None, "exp"),
        P("exp", None),
        P("exp"),
        P("grp", "exp", None),
        P("grp", "exp", None),
    )
    return jax.shard_map(
        on_device,
        mesh=mesh,
        in_specs=placed,
        out_specs=P("grp", None, None, "exp"),
        check_vma=False,
    )
```

```python
import functools

import jax
import jax.numpy as jnp
from jax import lax
from jax.experimental import pallas as pl
from jax.experimental.pallas import tpu as pltpu
from jax.sharding import PartitionSpec as P

HDIM = 128
EXPERTS = 64
FFE = 1408
TOPK = 6
BEAMS = 8
STEPS = 4
CAP_E = 3
HALF = 4
PREV = 60
LANES = 128
MODEL = 2048
ROWS = STEPS * HALF
PAIR = 2 * ROWS
STATS = 1 + TOPK

NEGATIVE = -1e30
EPSILON = 1e-06
MIB = 1024 * 1024
BF = jnp.bfloat16
HINT = 10**10
F32 = jnp.float32

VMEM = pl.BlockSpec(memory_space=pltpu.VMEM)
SMEM = pl.BlockSpec(memory_space=pltpu.SMEM)
ANY = pl.BlockSpec(memory_space=pl.ANY)


def iota(shape, dim):
    return lax.broadcasted_iota(jnp.int32, shape, dim)


def dot(a, b):
    return jnp.dot(a, b, preferred_element_type=F32)


def dot_t(a, b):
    return lax.dot_general(a, b, (((1,), (1,)), ((), ())), preferred_element_type=F32)


def t_dot(a, b):
    return lax.dot_general(a, b, (((0,), (0,)), ((), ())), preferred_element_type=F32)


def exchanged(value, axis, mask):
    pairs = [(source, source ^ mask) for source in range(lax.axis_size(axis))]
    return lax.ppermute(value, axis, pairs)


def call(body, outs, in_specs, *args, after=(), scratch=(), limit=8, flops=0, nbytes=0):
    count = len(args)

    def ordered(*refs):
        body(*refs[:count], *refs[count + len(after) :])

    return pl.pallas_call(
        ordered if after else body,
        out_shape=outs,
        in_specs=list(in_specs) + [ANY] * len(after),
        out_specs=jax.tree.map(lambda _: VMEM, outs),
        scratch_shapes=list(scratch),
        compiler_params=pltpu.CompilerParams(vmem_limit_bytes=limit * MIB),
        cost_estimate=pl.CostEstimate(flops=flops, bytes_accessed=nbytes, transcendentals=0),
    )(*args, *after)


def shape(dims, dtype):
    return jax.ShapeDtypeStruct(tuple(dims), dtype)


def columns_kernel(order, tail_at, new_at):
    half = lax.axis_index("grp") % 2
    to_row = iota(order.shape, 0)
    wanted = (to_row % ROWS // HALF) * BEAMS + (to_row // ROWS) * HALF + to_row % HALF
    order[...] = (iota(order.shape, 1) == wanted).astype(BF)
    column = iota(tail_at.shape, 0)
    tail_at[...] = (iota(tail_at.shape, 1) == half * HALF + column % HALF).astype(BF)
    column = iota(new_at.shape, 0)
    place = BEAMS + BEAMS * (column // HALF) + half * HALF + column % HALF
    new_at[...] = (iota(new_at.shape, 1) == place).astype(BF)


def slot_rows(source):
    return jnp.concatenate([source[step].astype(F32) for step in range(STEPS)], axis=0)


def feature_part(rows, features):
    me = lax.axis_index("exp")
    mine = rows[:, :features]
    for k in range(1, rows.shape[1] // features):
        mine = jnp.where(me == k, rows[:, k * features : (k + 1) * features], mine)
    return mine


def send_kernel(x_own, parents, routes, out):
    rows = slot_rows(x_own)
    depth = rows.shape[1]
    out[:, :depth] = rows.astype(BF)
    lane = iota((ROWS, LANES), 1)
    info = jnp.zeros((ROWS, LANES), F32)
    named = slot_rows(routes)
    for k in range(TOPK):
        info = jnp.where(lane == k, named[:, k : k + 1], info)
    same = iota((HALF, HALF), 0) == iota((HALF, HALF), 1)
    columns = [
        jnp.sum(
            jnp.where(same, parents[step : step + 1, :].astype(F32), 0.0), axis=1, keepdims=True
        )
        for step in range(STEPS)
    ]
    info = jnp.where(lane == TOPK, jnp.concatenate(columns, axis=0), info)
    out[:, depth:] = info.astype(BF)


def own_kernel(sent, wqkv, tk_raw, tv_raw, query, keys, values, part, tk, tv):
    rows = sent[:, : wqkv.shape[1]]
    part[...] = feature_part(rows.astype(F32), part.shape[1])
    for k, out in enumerate((query, keys, values)):
        out[...] = dot(rows, wqkv[k]).astype(BF)
    tk[...] = tk_raw[...].reshape(tk.shape)
    tv[...] = tv_raw[...].reshape(tv.shape)


def in_order(first, own, far):
    return jnp.concatenate([jnp.where(first, own, far), jnp.where(first, far, own)], axis=0)


def pieces(value, count):
    out = []
    for _ in range(count - 1):
        out.append(value.astype(BF).astype(F32))
        value = value - out[-1]
    return out + [value]


def attend_kernel(
    parts,
    order,
    tail_at,
    new_at,
    sent,
    came,
    query_own,
    part_own,
    wqkv,
    key_new,
    value_new,
    kp,
    vp,
    tk,
    tv,
    out,
    x_out,
    named,
):
    half = lax.axis_index("grp") % 2
    first = half == 0
    width = kp.shape[1]
    heads = width // HDIM
    depth = wqkv.shape[1]
    far_rows = came[:, :depth]
    part_far = feature_part(far_rows.astype(F32), part_own.shape[1])
    x_out[...] = in_order(first, part_own[...], part_far)
    names = in_order(first, sent[:, depth:].astype(F32), came[:, depth:].astype(F32))
    named[...] = names
    parents = names[:, TOPK : TOPK + 1]
    query_far = dot(far_rows, wqkv[0]).astype(BF)
    query = in_order(first, query_own[...], query_far)
    lane = iota((BEAMS, LANES), 1)
    beam = iota((BEAMS, LANES), 0)
    state = (lane == beam).astype(F32)
    states = []
    for step in range(STEPS):
        at = step * HALF
        parent = jnp.concatenate(
            [parents[at : at + HALF], parents[ROWS + at : ROWS + at + HALF]], axis=0
        )
        taken = jnp.zeros((BEAMS, LANES), F32)
        for j in range(BEAMS):
            taken = taken + jnp.where(parent == float(j), state[j : j + 1, :], 0.0)
        state = jnp.where(lane == BEAMS + BEAMS * step + beam, 1.0, taken)
        states.append(state)
    held = jnp.concatenate(states, axis=0).astype(BF)
    held = dot(order[...], held).astype(BF)
    held = jnp.concatenate([held] * heads, axis=0)
    spread = jnp.concatenate([query] * heads, axis=0)
    lanes = heads * PAIR
    owner = iota((lanes, width), 0) // PAIR == iota((lanes, width), 1) // HDIM
    spread = jnp.where(owner, spread.astype(F32), 0.0).astype(BF)
    cap = kp.shape[0]
    scale = HDIM ** (-0.5)
    live = iota((lanes, cap), 1) < parts[0]
    s_p = jnp.where(live, dot_t(spread, kp[...]) * scale, NEGATIVE)
    s_t = jnp.where(dot_t(held, tail_at[...]) > 0.5, dot_t(spread, tk[...]) * scale, NEGATIVE)
    s_n = jnp.where(
        dot_t(held, new_at[...]) > 0.5, dot_t(spread, key_new[...]) * scale, NEGATIVE
    )
    top = jnp.maximum(
        jnp.max(s_p, axis=1, keepdims=True),
        jnp.maximum(jnp.max(s_t, axis=1, keepdims=True), jnp.max(s_n, axis=1, keepdims=True)),
    )
    p_p, p_t, p_n = [jnp.exp(part - top) for part in (s_p, s_t, s_n)]
    total = (
        jnp.sum(p_p, axis=1, keepdims=True)
        + jnp.sum(p_t, axis=1, keepdims=True)
        + jnp.sum(p_n, axis=1, keepdims=True)
    )
    mix = (
        dot(p_p.astype(BF), vp[...])
        + dot(p_t.astype(BF), tv[...])
        + dot(p_n.astype(BF), value_new[...])
    )
    info = jnp.zeros((PAIR, LANES), F32)
    info_lane = iota((PAIR, LANES), 1)
    for head in range(heads):
        at = slice(head * HDIM, (head + 1) * HDIM)
        these = slice(head * PAIR, (head + 1) * PAIR)
        out[:, at] = mix[these, at].astype(BF)
        for k, column in enumerate(pieces(top[these], 3) + pieces(total[these], 2)):
            info = jnp.where(info_lane == k * heads + head, column, info)
    out[:, width:] = info.astype(BF)


def project_kernel(near, far, w_out, *outs):
    me = lax.axis_index("exp")
    width = w_out.shape[0]
    heads = width // HDIM
    parts = []
    infos = [side[:, width:].astype(F32) for side in (near, far)]
    for head in range(heads):
        at = slice(head * HDIM, (head + 1) * HDIM)
        columns = [
            [info[:, k * heads + head : k * heads + head + 1] for k in range(5)] for info in infos
        ]
        (m_near, l_near), (m_far, l_far) = [
            ((c[0] + c[1]) + c[2], c[3] + c[4]) for c in columns
        ]
        top = jnp.maximum(m_near, m_far)
        f_near = jnp.exp(m_near - top)
        f_far = jnp.exp(m_far - top)
        total = l_near * f_near + l_far * f_far
        mix = near[:, at].astype(F32) * f_near + far[:, at].astype(F32) * f_far
        parts.append((mix / total).astype(BF))
    attention = jnp.concatenate(parts, axis=1)
    features = outs[0].shape[1]
    for k, out in enumerate(outs):
        start = pl.multiple_of((me ^ k) * features, LANES)
        out[...] = dot(attention, w_out[:, pl.ds(start, features)]).astype(out.dtype)


def residual_kernel(x, named, gain, w_router, own, *rest):
    others, (residual_out, message) = rest[:-2], rest[-2:]
    features = own.shape[1]
    residual = x[...] + own[...]
    for other in others:
        residual = residual + other[...].astype(F32)
    residual_out[...] = residual
    rows = (residual * gain[...]).astype(BF)
    message[:, :features] = rows
    logits = dot_t(rows, w_router[...])
    expert = iota(logits.shape, 1).astype(F32)
    lane = iota((PAIR, LANES), 1)
    info = jnp.zeros((PAIR, LANES), F32)
    columns = [jnp.sum(residual * residual, axis=1, keepdims=True)]
    for k in range(TOPK):
        route = named[:, k : k + 1]
        columns.append(jnp.sum(jnp.where(expert == route, logits, 0.0), axis=1, keepdims=True))
        info = jnp.where(lane == 2 * STATS + k, route, info)
    for at, column in enumerate(columns):
        high = column.astype(BF).astype(F32)
        info = jnp.where(lane == at, high, info)
        info = jnp.where(lane == STATS + at, column - high, info)
    message[:, features:] = info.astype(BF)


def gather_kernel(local, *refs):
    messages, (picked, stats, target, choice, rows) = refs[:-5], refs[-5:]
    blocks = len(messages)
    tokens = blocks * PAIR
    features = rows.shape[1]
    parts = []
    for k, message in enumerate(messages):
        rows[k * PAIR : (k + 1) * PAIR, :] = message[:, :features]
        parts.append(message[:, features:].astype(F32))
    info = jnp.concatenate(parts, axis=0).T
    stats[...] = jnp.concatenate(
        [info[:STATS] + info[STATS : 2 * STATS], jnp.zeros((8 - STATS, tokens), F32)], axis=0
    )
    first = (lax.axis_index("grp") * local).astype(F32)
    expert = iota((8, tokens), 0).astype(F32)
    chosen = jnp.full((8, tokens), -1.0, F32)
    for k in range(TOPK):
        route = info[2 * STATS + k : 2 * STATS + k + 1] - first
        chosen = jnp.where((route == expert) & (expert < local), float(k), chosen)
    choice[...] = chosen
    named = chosen >= 0.0
    before = iota((tokens, tokens), 0)
    after = iota((tokens, tokens), 1)
    earlier = ((before < after) & (before // ROWS == after // ROWS)).astype(BF)
    rank = dot(named.astype(BF), earlier)
    slot = (iota((8, tokens), 1) // ROWS).astype(F32)
    goal = jnp.where(named, slot * CAP_E + rank, -1.0)
    target[...] = goal
    capacity = picked.shape[1]
    row = iota((capacity, tokens), 0).astype(F32)
    places = [(row == goal[e : e + 1]).astype(F32) for e in range(local)]
    result = dot(jnp.concatenate(places, axis=0).astype(BF), rows[...])
    for e in range(local):
        picked[e] = result[e * capacity : (e + 1) * capacity].astype(BF)


def split_rows(value, rows):
    high = value[:STATS].astype(BF).astype(F32)
    low = value[:STATS] - high
    rest = jnp.zeros((rows - 2 * STATS, value.shape[1]), F32)
    return jnp.concatenate([high, low, rest], axis=0).astype(BF)


def joined_rows(value):
    value = value.astype(F32)
    high, low = value[:STATS], value[STATS : 2 * STATS]
    return jnp.concatenate([high + low, jnp.zeros((8 - STATS, value.shape[1]), F32)], axis=0)


def gate_kernel(places, block, with_stats, count, weights, picked, *refs):
    if with_stats:
        stats, refs = refs[0], refs[1:]
    far, outs = refs[:count], refs[count:]
    me = lax.axis_index("exp")
    width = weights.shape[2]
    for i, (mask, pick) in enumerate(places):
        at = (me ^ mask) * block + pick
        result = dot(picked[at], weights[at])
        if far:
            result = result + far[i][:, :width].astype(F32)
        outs[i][:, :width] = result.astype(outs[i].dtype)
    if with_stats:
        value = stats[...]
        if far:
            value = value + joined_rows(far[0][:, width:])
            outs[-1][...] = value
        outs[0][:, width:] = split_rows(value, outs[0].shape[0])


def gate_block(places, weights, picked, block, stats=(), far=(), dtypes=(BF,), after=(), flops=0):
    capacity, depth = picked.shape[1:]
    width = weights.shape[2]
    outs = [shape((capacity, width), dtype) for dtype in dtypes]
    if stats:
        outs[0] = shape((capacity, width + stats[0].shape[1]), BF)
        if far:
            outs.append(shape(stats[0].shape, F32))
    return call(
        functools.partial(gate_kernel, places, block, bool(stats), len(far)),
        tuple(outs),
        [VMEM] * (2 + len(stats) + len(far)),
        weights,
        picked,
        *stats,
        *far,
        after=after,
        flops=flops,
    )


def place_kernel(local, target, choice, stats, far, shared):
    stats = stats[...] + joined_rows(far[:, far.shape[1] - target.shape[1] :])
    inverse = lax.rsqrt(stats[0:1] / MODEL + EPSILON)
    logits = [stats[1 + k : 2 + k] * inverse for k in range(TOPK)]
    top = functools.reduce(jnp.maximum, logits)
    weights = [jnp.exp(logit - top) for logit in logits]
    whole = functools.reduce(lambda a, b: a + b, weights)
    chosen = choice[...]
    share = jnp.zeros(chosen.shape, F32)
    for k in range(TOPK):
        share = jnp.where(chosen == float(k), weights[k] / whole, share)
    capacity = shared.shape[2] // 2
    row = iota((capacity, target.shape[1]), 0).astype(F32)
    for e in range(local):
        place = jnp.where(row == target[e : e + 1, :], share[e : e + 1], 0.0)
        high = place.astype(BF).astype(F32)
        shared[e] = jnp.concatenate([high, place - high], axis=0).T.astype(BF)


def hidden_kernel(block, pick, near, mid, far, target, stats, far_stats, hidden):
    capacity = near.shape[0]
    stats = stats[...] + joined_rows(far_stats[:, far_stats.shape[1] - target.shape[1] :])
    inverse = lax.rsqrt(stats[0:1] / MODEL + EPSILON)
    goal = target[pl.ds(lax.axis_index("exp") * block + pick, 1), :]
    row = iota((capacity, target.shape[1]), 0).astype(F32)
    scale = jnp.sum(jnp.where(row == goal, inverse, 0.0), axis=1, keepdims=True)
    half = near.shape[1] // 2
    gate = near[:, :half] + mid[:, :half].astype(F32) + far[:, :half].astype(F32)
    up = near[:, half:] + mid[:, half:].astype(F32) + far[:, half : 2 * half].astype(F32)
    gate, up = gate * scale, up * scale
    hidden[...] = (gate / (1.0 + jnp.exp(-gate)) * up).astype(BF)


def down_kernel(places, block, last, count, weights, shared, *refs):
    hiddens, refs = refs[: len(places)], refs[len(places) :]
    before, refs = refs[:count], refs[count:]
    me = lax.axis_index("exp")
    mixed = before[0][...] if before else 0.0
    for hidden, (mask, pick) in zip(hiddens, places):
        at = (me ^ mask) * block + pick
        result = dot_t(hidden[...], weights[at]).astype(BF).astype(F32)
        result = jnp.concatenate([result, result], axis=0).astype(BF)
        mixed = mixed + dot(shared[at], result)
    if not last:
        refs[0][...] = mixed
        return
    keep, send, last_send = refs
    first = lax.axis_index("grp") % 2 == 0
    for k in range(keep.shape[0]):
        low = mixed[k * PAIR : k * PAIR + ROWS]
        high = mixed[k * PAIR + ROWS : (k + 1) * PAIR]
        keep[k] = jnp.where(first, low, high)
        given = jnp.where(first, high, low).astype(BF)
        if k:
            send[k - 1] = given
        else:
            last_send[...] = given


def down_blocks(places, hiddens, weights, shared, block, before=(), last=False, after=()):
    features, width = weights.shape[1:]
    tokens = shared.shape[1]
    if last:
        count = tokens // PAIR
        out = (
            shape((count, ROWS, features), F32),
            shape((count - 1, ROWS, features), BF),
            shape((ROWS, features), BF),
        )
    else:
        out = shape((tokens, features), F32)
    return call(
        functools.partial(down_kernel, places, block, last, len(before)),
        out,
        [VMEM] * (2 + len(hiddens) + len(before)),
        weights,
        shared,
        *hiddens,
        *before,
        after=after,
    )


def fold_kernel(keep, far, *outs):
    for k, out in enumerate(outs):
        out[...] = (keep[k + 1] + far[k].astype(F32)).astype(out.dtype)


def finish_kernel(residual, keep, far, *rest):
    others, out = rest[:-1], rest[-1]
    half = lax.axis_index("grp") % 2
    value = residual[pl.ds(pl.multiple_of(half * ROWS, ROWS), ROWS), :] + keep[0] + far[...].astype(F32)
    for other in others:
        value = value + other[...].astype(F32)
    out[...] = value.astype(out.dtype)


def on_device(
    step_inputs,
    parents,
    routes,
    w_qkv,
    w_out,
    prompt_keys,
    prompt_values,
    prompt_parts,
    tail_keys,
    tail_values,
    w_router,
    norm_gain,
    w_gate_up,
    w_down,
):
    groups = lax.axis_size("grp")
    splits = lax.axis_size("exp")
    requests = groups // 2
    model = w_qkv.shape[0]
    width = w_qkv.shape[2]
    features = norm_gain.shape[0]
    local = w_gate_up.shape[0]
    tokens = requests * PAIR

    w_all = w_qkv.transpose(1, 0, 2)
    columns = call(
        columns_kernel,
        (
            shape((PAIR, PAIR), BF),
            shape((PREV * HALF, LANES), BF),
            shape((ROWS, LANES), BF),
        ),
        [],
        flops=HINT,
    )
    sent = call(
        send_kernel,
        shape((ROWS, model + LANES), BF),
        [VMEM] * 3,
        step_inputs[0],
        parents[0],
        routes[0],
        after=columns[:1],
    )
    came = exchanged(sent, "grp", 1)
    query, keys_new, values_new, part, tail_k, tail_v = call(
        own_kernel,
        (shape((ROWS, width), BF),) * 3
        + (shape((ROWS, features), F32),)
        + (shape((PREV * HALF, width), BF),) * 2,
        [VMEM] * 4,
        sent,
        w_all,
        tail_keys[0].transpose(1, 0, 2),
        tail_values[0].transpose(1, 0, 2),
        flops=HINT // 4,
    )
    near, x, named = call(
        attend_kernel,
        (
            shape((PAIR, width + LANES), BF),
            shape((PAIR, features), F32),
            shape((PAIR, LANES), F32),
        ),
        [SMEM] + [VMEM] * 14,
        prompt_parts,
        *columns,
        sent,
        came,
        query,
        part,
        w_all,
        keys_new,
        values_new,
        prompt_keys[0],
        prompt_values[0],
        tail_k,
        tail_v,
        flops=HINT,
    )
    far = exchanged(near, "grp", 1)
    terms = call(
        project_kernel,
        tuple(shape((PAIR, features), F32 if k == 0 else BF) for k in range(splits)),
        [VMEM] * 3,
        near,
        far,
        w_out,
        flops=HINT,
    )
    arrived = [exchanged(terms[k], "exp", k) for k in range(1, splits)]
    residual, message = call(
        residual_kernel,
        (shape((PAIR, features), F32), shape((PAIR, features + LANES), BF)),
        [VMEM] * (5 + len(arrived)),
        x,
        named,
        norm_gain.reshape(1, features),
        w_router.T,
        terms[0],
        *arrived,
        flops=HINT,
    )
    messages = [exchanged(message, "grp", 2 * k) for k in range(1, requests)]
    messages = [message] + messages
    picked, stats, target, choice = call(
        functools.partial(gather_kernel, local),
        (
            shape((local, EXPERTS * CAP_E // local, features), BF),
            shape((8, tokens), F32),
            shape((8, tokens), F32),
            shape((8, tokens), F32),
        ),
        [VMEM] * requests,
        *messages,
        scratch=[pltpu.VMEM((tokens, features), BF)],
        flops=HINT,
    )
    if splits == 4 and local == 2 * splits:
        gate = functools.partial(gate_block, weights=w_gate_up, picked=picked, block=2)
        (a0,) = gate(((3, 0),), stats=(stats,))
        far_a0 = exchanged(a0, "exp", 1)
        (a1,) = gate(((3, 1),), after=(a0,))
        far_a1 = exchanged(a1, "exp", 1)
        c0, stats = gate(((2, 0),), stats=(stats,), far=(far_a0,), after=(a1,))
        far_c0 = exchanged(c0, "exp", 2)
        (c1,) = gate(((2, 1),), far=(far_a1,), after=(c0,))
        far_c1 = exchanged(c1, "exp", 2)
        b0, d0 = gate(((1, 0), (0, 0)), dtypes=(BF, F32), after=(c1,), flops=30 * HINT // 100)
        far_b0 = exchanged(b0, "exp", 1)
        b1, d1 = gate(((1, 1), (0, 1)), dtypes=(BF, F32), after=(d0,), flops=30 * HINT // 100)
        far_b1 = exchanged(b1, "exp", 1)

        def hidden_of(pick, near, mid, far, after=()):
            return call(
                functools.partial(hidden_kernel, 2, pick),
                shape((near.shape[0], FFE), BF),
                [VMEM] * 6,
                near,
                mid,
                far,
                target,
                stats,
                far_c0,
                after=after,
                flops=10 * HINT // 100,
            )

        own0 = hidden_of(0, d0, far_b0, far_c0, after=(d1,))
        core0 = exchanged(own0, "exp", 1)
        y0 = exchanged(own0, "exp", 2)
        shared = call(
            functools.partial(place_kernel, local),
            shape((local, tokens, 2 * picked.shape[1]), BF),
            [VMEM] * 4,
            target,
            choice,
            stats,
            far_c0,
            after=(own0,),
            flops=10 * HINT // 100,
        )
        down = functools.partial(down_blocks, weights=w_down, shared=shared, block=2)
        own1 = hidden_of(1, d1, far_b1, far_c1, after=(shared,))
        core1 = exchanged(own1, "exp", 1)
        y1 = exchanged(own1, "exp", 2)
        mixed = down(((0, 0), (1, 0)), (own0, core0), after=(own1,))
        y0, mixed = lax.optimization_barrier((y0, mixed))
        far0 = exchanged(y0, "exp", 1)
        mixed = down(((0, 1), (1, 1), (2, 0)), (own1, core1, y0), before=(mixed,))
        y1, mixed = lax.optimization_barrier((y1, mixed))
        far1 = exchanged(y1, "exp", 1)
        mixed = down(((3, 0), (2, 1)), (far0, y1), before=(mixed,))
        keep, send, last_send = down(((3, 1),), (far1,), before=(mixed,), last=True)
    else:
        stats = lax.psum(stats, "exp")
        sums = jnp.einsum("lcd,ldf->lcf", picked, w_gate_up, preferred_element_type=F32)
        sums = lax.psum(sums.astype(BF), "exp").astype(F32)
        inverse = lax.rsqrt(stats[0] / model + EPSILON)
        goal, pick = target[:local], choice[:local]
        place = goal[:, None, :] == jnp.arange(picked.shape[1], dtype=F32)[None, :, None]
        sums = sums * jnp.sum(jnp.where(place, inverse, 0.0), axis=2, keepdims=True)
        hidden = (jax.nn.silu(sums[..., :FFE]) * sums[..., FFE:]).astype(BF)
        result = jnp.einsum("lcf,ldf->lcd", hidden, w_down, preferred_element_type=F32)
        share = jax.nn.softmax(stats[1:STATS] * inverse, axis=0)
        ids = jnp.arange(TOPK, dtype=F32)[None, :, None]
        weight = jnp.sum(jnp.where(pick[:, None, :] == ids, share[None], 0.0), axis=1)
        mixed = jnp.einsum(
            "lct,lcd->td",
            jnp.where(place, weight[:, None, :], 0.0),
            result.astype(BF).astype(F32),
            precision=lax.Precision.HIGHEST,
        )
        mixed = mixed.reshape(requests, 2, ROWS, features)
        half = lax.axis_index("grp") % 2
        keep = lax.dynamic_index_in_dim(mixed, half, 1, False)
        send = lax.dynamic_index_in_dim(mixed, 1 - half, 1, False).astype(BF)
        send, last_send = send[1:], send[0]
    folded = call(
        fold_kernel,
        tuple(shape((ROWS, features), BF) for _ in range(1, requests)),
        [VMEM] * 2,
        keep,
        exchanged(send, "grp", 1),
    )
    back = [exchanged(folded[k - 1], "grp", 2 * k) for k in range(1, requests)]
    result = call(
        finish_kernel,
        shape((ROWS, features), BF),
        [VMEM] * (3 + len(back)),
        residual,
        keep,
        exchanged(last_send, "grp", 1),
        *back[::-1],
    )
    return result.reshape(1, STEPS, HALF, features)


def solution(mesh):
    placed = (
        P("grp", None, None, None),
        P("grp", None, None),
        P("grp", None, None, None),
        P(None, None, "exp"),
        P("exp", None),
        P("grp", None, "exp"),
        P("grp", None, "exp"),
        P("grp"),
        P("grp", None, None, "exp"),
        P("grp", None, None, "exp"),
        P("exp", None),
        P("exp"),
        P("grp", "exp", None),
        P("grp", "exp", None),
    )
    return jax.shard_map(
        on_device,
        mesh=mesh,
        in_specs=placed,
        out_specs=P("grp", None, None, "exp"),
        check_vma=False,
    )
```

```python
import functools

import jax
import jax.numpy as jnp
from jax import lax
from jax.experimental import pallas as pl
from jax.experimental.pallas import tpu as pltpu
from jax.sharding import PartitionSpec as P

HDIM = 128
EXPERTS = 64
FFE = 1408
TOPK = 6
BEAMS = 8
STEPS = 4
CAP_E = 3
HALF = 4
PREV = 60
LANES = 128
MODEL = 2048
ROWS = STEPS * HALF
PAIR = 2 * ROWS
STATS = 1 + TOPK

NEGATIVE = -1e30
EPSILON = 1e-06
MIB = 1024 * 1024
BF = jnp.bfloat16
HINT = 10**10
F32 = jnp.float32

VMEM = pl.BlockSpec(memory_space=pltpu.VMEM)
SMEM = pl.BlockSpec(memory_space=pltpu.SMEM)
ANY = pl.BlockSpec(memory_space=pl.ANY)


def iota(shape, dim):
    return lax.broadcasted_iota(jnp.int32, shape, dim)


def dot(a, b):
    return jnp.dot(a, b, preferred_element_type=F32)


def dot_t(a, b):
    return lax.dot_general(a, b, (((1,), (1,)), ((), ())), preferred_element_type=F32)


def t_dot(a, b):
    return lax.dot_general(a, b, (((0,), (0,)), ((), ())), preferred_element_type=F32)


def exchanged(value, axis, mask):
    pairs = [(source, source ^ mask) for source in range(lax.axis_size(axis))]
    return lax.ppermute(value, axis, pairs)


def call(body, outs, in_specs, *args, after=(), scratch=(), limit=8, flops=0, nbytes=0):
    count = len(args)

    def ordered(*refs):
        body(*refs[:count], *refs[count + len(after) :])

    return pl.pallas_call(
        ordered if after else body,
        out_shape=outs,
        in_specs=list(in_specs) + [ANY] * len(after),
        out_specs=jax.tree.map(lambda _: VMEM, outs),
        scratch_shapes=list(scratch),
        compiler_params=pltpu.CompilerParams(vmem_limit_bytes=limit * MIB),
        cost_estimate=pl.CostEstimate(flops=flops, bytes_accessed=nbytes, transcendentals=0),
    )(*args, *after)


def shape(dims, dtype):
    return jax.ShapeDtypeStruct(tuple(dims), dtype)


def columns_kernel(order, tail_at, new_at):
    half = lax.axis_index("grp") % 2
    to_row = iota(order.shape, 0)
    wanted = (to_row % ROWS // HALF) * BEAMS + (to_row // ROWS) * HALF + to_row % HALF
    order[...] = (iota(order.shape, 1) == wanted).astype(BF)
    column = iota(tail_at.shape, 0)
    tail_at[...] = (iota(tail_at.shape, 1) == half * HALF + column % HALF).astype(BF)
    column = iota(new_at.shape, 0)
    place = BEAMS + BEAMS * (column // HALF) + half * HALF + column % HALF
    new_at[...] = (iota(new_at.shape, 1) == place).astype(BF)


def slot_rows(source):
    return jnp.concatenate([source[step].astype(F32) for step in range(STEPS)], axis=0)


def feature_part(rows, features):
    me = lax.axis_index("exp")
    mine = rows[:, :features]
    for k in range(1, rows.shape[1] // features):
        mine = jnp.where(me == k, rows[:, k * features : (k + 1) * features], mine)
    return mine


def send_kernel(x_own, parents, routes, out):
    rows = slot_rows(x_own)
    depth = rows.shape[1]
    out[:, :depth] = rows.astype(BF)
    lane = iota((ROWS, LANES), 1)
    info = jnp.zeros((ROWS, LANES), F32)
    named = slot_rows(routes)
    for k in range(TOPK):
        info = jnp.where(lane == k, named[:, k : k + 1], info)
    same = iota((HALF, HALF), 0) == iota((HALF, HALF), 1)
    columns = [
        jnp.sum(
            jnp.where(same, parents[step : step + 1, :].astype(F32), 0.0), axis=1, keepdims=True
        )
        for step in range(STEPS)
    ]
    info = jnp.where(lane == TOPK, jnp.concatenate(columns, axis=0), info)
    out[:, depth:] = info.astype(BF)


def own_kernel(sent, wqkv, tk_raw, tv_raw, query, keys, values, part, tk, tv):
    rows = sent[:, : wqkv.shape[1]]
    part[...] = feature_part(rows.astype(F32), part.shape[1])
    for k, out in enumerate((query, keys, values)):
        out[...] = dot(rows, wqkv[k]).astype(BF)
    tk[...] = tk_raw[...].reshape(tk.shape)
    tv[...] = tv_raw[...].reshape(tv.shape)


def in_order(first, own, far):
    return jnp.concatenate([jnp.where(first, own, far), jnp.where(first, far, own)], axis=0)


def pieces(value, count):
    out = []
    for _ in range(count - 1):
        out.append(value.astype(BF).astype(F32))
        value = value - out[-1]
    return out + [value]


def attend_kernel(
    parts,
    order,
    tail_at,
    new_at,
    sent,
    came,
    query_own,
    part_own,
    wqkv,
    key_new,
    value_new,
    kp,
    vp,
    tk,
    tv,
    out,
    x_out,
    named,
):
    half = lax.axis_index("grp") % 2
    first = half == 0
    width = kp.shape[1]
    heads = width // HDIM
    depth = wqkv.shape[1]
    far_rows = came[:, :depth]
    part_far = feature_part(far_rows.astype(F32), part_own.shape[1])
    x_out[...] = in_order(first, part_own[...], part_far)
    names = in_order(first, sent[:, depth:].astype(F32), came[:, depth:].astype(F32))
    named[...] = names
    parents = names[:, TOPK : TOPK + 1]
    query_far = dot(far_rows, wqkv[0]).astype(BF)
    query = in_order(first, query_own[...], query_far)
    lane = iota((BEAMS, LANES), 1)
    beam = iota((BEAMS, LANES), 0)
    state = (lane == beam).astype(F32)
    states = []
    for step in range(STEPS):
        at = step * HALF
        parent = jnp.concatenate(
            [parents[at : at + HALF], parents[ROWS + at : ROWS + at + HALF]], axis=0
        )
        taken = jnp.zeros((BEAMS, LANES), F32)
        for j in range(BEAMS):
            taken = taken + jnp.where(parent == float(j), state[j : j + 1, :], 0.0)
        state = jnp.where(lane == BEAMS + BEAMS * step + beam, 1.0, taken)
        states.append(state)
    held = jnp.concatenate(states, axis=0).astype(BF)
    held = dot(order[...], held).astype(BF)
    held = jnp.concatenate([held] * heads, axis=0)
    spread = jnp.concatenate([query] * heads, axis=0)
    lanes = heads * PAIR
    owner = iota((lanes, width), 0) // PAIR == iota((lanes, width), 1) // HDIM
    spread = jnp.where(owner, spread.astype(F32), 0.0).astype(BF)
    cap = kp.shape[0]
    scale = HDIM ** (-0.5)
    live = iota((lanes, cap), 1) < parts[0]
    s_p = jnp.where(live, dot_t(spread, kp[...]) * scale, NEGATIVE)
    s_t = jnp.where(dot_t(held, tail_at[...]) > 0.5, dot_t(spread, tk[...]) * scale, NEGATIVE)
    s_n = jnp.where(
        dot_t(held, new_at[...]) > 0.5, dot_t(spread, key_new[...]) * scale, NEGATIVE
    )
    top = jnp.maximum(
        jnp.max(s_p, axis=1, keepdims=True),
        jnp.maximum(jnp.max(s_t, axis=1, keepdims=True), jnp.max(s_n, axis=1, keepdims=True)),
    )
    p_p, p_t, p_n = [jnp.exp(part - top) for part in (s_p, s_t, s_n)]
    total = (
        jnp.sum(p_p, axis=1, keepdims=True)
        + jnp.sum(p_t, axis=1, keepdims=True)
        + jnp.sum(p_n, axis=1, keepdims=True)
    )
    mix = (
        dot(p_p.astype(BF), vp[...])
        + dot(p_t.astype(BF), tv[...])
        + dot(p_n.astype(BF), value_new[...])
    )
    info = jnp.zeros((PAIR, LANES), F32)
    info_lane = iota((PAIR, LANES), 1)
    for head in range(heads):
        at = slice(head * HDIM, (head + 1) * HDIM)
        these = slice(head * PAIR, (head + 1) * PAIR)
        out[:, at] = mix[these, at].astype(BF)
        for k, column in enumerate(pieces(top[these], 3) + pieces(total[these], 2)):
            info = jnp.where(info_lane == k * heads + head, column, info)
    out[:, width:] = info.astype(BF)


def project_kernel(masks, near, far, w_out, joined, *outs):
    width = w_out.shape[0]
    heads = width // HDIM
    parts = []
    infos = [side[:, width:].astype(F32) for side in (near, far)]
    for head in range(heads):
        at = slice(head * HDIM, (head + 1) * HDIM)
        columns = [
            [info[:, k * heads + head : k * heads + head + 1] for k in range(5)] for info in infos
        ]
        (m_near, l_near), (m_far, l_far) = [
            ((c[0] + c[1]) + c[2], c[3] + c[4]) for c in columns
        ]
        top = jnp.maximum(m_near, m_far)
        f_near = jnp.exp(m_near - top)
        f_far = jnp.exp(m_far - top)
        total = l_near * f_near + l_far * f_far
        mix = near[:, at].astype(F32) * f_near + far[:, at].astype(F32) * f_far
        parts.append((mix / total).astype(BF))
    attention = jnp.concatenate(parts, axis=1)
    joined[...] = attention
    project_blocks(masks, attention, w_out, outs)


def project_blocks(masks, attention, w_out, outs):
    me = lax.axis_index("exp")
    features = outs[0].shape[1]
    for mask, out in zip(masks, outs):
        start = pl.multiple_of((me ^ mask) * features, LANES)
        out[...] = dot(attention, w_out[:, pl.ds(start, features)]).astype(out.dtype)


def near_kernel(masks, joined, w_out, *outs):
    project_blocks(masks, joined[...], w_out, outs)


def residual_kernel(x, named, gain, w_router, own, *rest):
    others, (residual_out, message) = rest[:-2], rest[-2:]
    features = own.shape[1]
    residual = x[...] + own[...]
    for other in others:
        residual = residual + other[...].astype(F32)
    residual_out[...] = residual
    rows = (residual * gain[...]).astype(BF)
    message[:, :features] = rows
    logits = dot_t(rows, w_router[...])
    expert = iota(logits.shape, 1).astype(F32)
    lane = iota((PAIR, LANES), 1)
    info = jnp.zeros((PAIR, LANES), F32)
    columns = [jnp.sum(residual * residual, axis=1, keepdims=True)]
    for k in range(TOPK):
        route = named[:, k : k + 1]
        columns.append(jnp.sum(jnp.where(expert == route, logits, 0.0), axis=1, keepdims=True))
        info = jnp.where(lane == 2 * STATS + k, route, info)
    for at, column in enumerate(columns):
        high = column.astype(BF).astype(F32)
        info = jnp.where(lane == at, high, info)
        info = jnp.where(lane == STATS + at, column - high, info)
    message[:, features:] = info.astype(BF)


def gather_kernel(local, *refs):
    messages, (picked, stats, target, choice, rows) = refs[:-5], refs[-5:]
    blocks = len(messages)
    tokens = blocks * PAIR
    features = rows.shape[1]
    parts = []
    for k, message in enumerate(messages):
        rows[k * PAIR : (k + 1) * PAIR, :] = message[:, :features]
        parts.append(message[:, features:].astype(F32))
    info = jnp.concatenate(parts, axis=0).T
    stats[...] = jnp.concatenate(
        [info[:STATS] + info[STATS : 2 * STATS], jnp.zeros((8 - STATS, tokens), F32)], axis=0
    )
    first = (lax.axis_index("grp") * local).astype(F32)
    expert = iota((8, tokens), 0).astype(F32)
    chosen = jnp.full((8, tokens), -1.0, F32)
    for k in range(TOPK):
        route = info[2 * STATS + k : 2 * STATS + k + 1] - first
        chosen = jnp.where((route == expert) & (expert < local), float(k), chosen)
    choice[...] = chosen
    named = chosen >= 0.0
    before = iota((tokens, tokens), 0)
    after = iota((tokens, tokens), 1)
    earlier = ((before < after) & (before // ROWS == after // ROWS)).astype(BF)
    rank = dot(named.astype(BF), earlier)
    slot = (iota((8, tokens), 1) // ROWS).astype(F32)
    goal = jnp.where(named, slot * CAP_E + rank, -1.0)
    target[...] = goal
    capacity = picked.shape[1]
    row = iota((capacity, tokens), 0).astype(F32)
    places = [(row == goal[e : e + 1]).astype(F32) for e in range(local)]
    result = dot(jnp.concatenate(places, axis=0).astype(BF), rows[...])
    for e in range(local):
        picked[e] = result[e * capacity : (e + 1) * capacity].astype(BF)


def split_rows(value, rows):
    high = value[:STATS].astype(BF).astype(F32)
    low = value[:STATS] - high
    rest = jnp.zeros((rows - 2 * STATS, value.shape[1]), F32)
    return jnp.concatenate([high, low, rest], axis=0).astype(BF)


def joined_rows(value):
    value = value.astype(F32)
    high, low = value[:STATS], value[STATS : 2 * STATS]
    return jnp.concatenate([high + low, jnp.zeros((8 - STATS, value.shape[1]), F32)], axis=0)


def gate_kernel(places, block, with_stats, count, weights, picked, *refs):
    if with_stats:
        stats, refs = refs[0], refs[1:]
    far, outs = refs[:count], refs[count:]
    me = lax.axis_index("exp")
    width = weights.shape[2]
    for i, (mask, pick) in enumerate(places):
        at = (me ^ mask) * block + pick
        result = dot(picked[at], weights[at])
        if far:
            result = result + far[i][:, :width].astype(F32)
        outs[i][:, :width] = result.astype(outs[i].dtype)
    if with_stats:
        value = stats[...]
        if far:
            value = value + joined_rows(far[0][:, width:])
            outs[-1][...] = value
        outs[0][:, width:] = split_rows(value, outs[0].shape[0])


def gate_block(places, weights, picked, block, stats=(), far=(), dtypes=(BF,), after=(), flops=0):
    capacity, depth = picked.shape[1:]
    width = weights.shape[2]
    outs = [shape((capacity, width), dtype) for dtype in dtypes]
    if stats:
        outs[0] = shape((capacity, width + stats[0].shape[1]), BF)
        if far:
            outs.append(shape(stats[0].shape, F32))
    return call(
        functools.partial(gate_kernel, places, block, bool(stats), len(far)),
        tuple(outs),
        [VMEM] * (2 + len(stats) + len(far)),
        weights,
        picked,
        *stats,
        *far,
        after=after,
        flops=flops,
    )


def place_kernel(local, target, choice, stats, far, shared):
    stats = stats[...] + joined_rows(far[:, far.shape[1] - target.shape[1] :])
    inverse = lax.rsqrt(stats[0:1] / MODEL + EPSILON)
    logits = [stats[1 + k : 2 + k] * inverse for k in range(TOPK)]
    top = functools.reduce(jnp.maximum, logits)
    weights = [jnp.exp(logit - top) for logit in logits]
    whole = functools.reduce(lambda a, b: a + b, weights)
    chosen = choice[...]
    share = jnp.zeros(chosen.shape, F32)
    for k in range(TOPK):
        share = jnp.where(chosen == float(k), weights[k] / whole, share)
    capacity = shared.shape[2] // 2
    row = iota((capacity, target.shape[1]), 0).astype(F32)
    for e in range(local):
        place = jnp.where(row == target[e : e + 1, :], share[e : e + 1], 0.0)
        high = place.astype(BF).astype(F32)
        shared[e] = jnp.concatenate([high, place - high], axis=0).T.astype(BF)


def hidden_kernel(block, pick, near, mid, far, target, stats, far_stats, hidden):
    capacity = near.shape[0]
    stats = stats[...] + joined_rows(far_stats[:, far_stats.shape[1] - target.shape[1] :])
    inverse = lax.rsqrt(stats[0:1] / MODEL + EPSILON)
    goal = target[pl.ds(lax.axis_index("exp") * block + pick, 1), :]
    row = iota((capacity, target.shape[1]), 0).astype(F32)
    scale = jnp.sum(jnp.where(row == goal, inverse, 0.0), axis=1, keepdims=True)
    half = near.shape[1] // 2
    gate = near[:, :half] + mid[:, :half].astype(F32) + far[:, :half].astype(F32)
    up = near[:, half:] + mid[:, half:].astype(F32) + far[:, half : 2 * half].astype(F32)
    gate, up = gate * scale, up * scale
    hidden[...] = (gate / (1.0 + jnp.exp(-gate)) * up).astype(BF)


def down_kernel(places, block, last, count, weights, shared, *refs):
    hiddens, refs = refs[: len(places)], refs[len(places) :]
    before, refs = refs[:count], refs[count:]
    me = lax.axis_index("exp")
    mixed = before[0][...] if before else 0.0
    for hidden, (mask, pick) in zip(hiddens, places):
        at = (me ^ mask) * block + pick
        result = dot_t(hidden[...], weights[at]).astype(BF).astype(F32)
        result = jnp.concatenate([result, result], axis=0).astype(BF)
        mixed = mixed + dot(shared[at], result)
    if not last:
        refs[0][...] = mixed
        return
    keep, send, last_send = refs
    first = lax.axis_index("grp") % 2 == 0
    for k in range(keep.shape[0]):
        low = mixed[k * PAIR : k * PAIR + ROWS]
        high = mixed[k * PAIR + ROWS : (k + 1) * PAIR]
        keep[k] = jnp.where(first, low, high)
        given = jnp.where(first, high, low).astype(BF)
        if k:
            send[k - 1] = given
        else:
            last_send[...] = given


def down_blocks(places, hiddens, weights, shared, block, before=(), last=False, after=()):
    features, width = weights.shape[1:]
    tokens = shared.shape[1]
    if last:
        count = tokens // PAIR
        out = (
            shape((count, ROWS, features), F32),
            shape((count - 1, ROWS, features), BF),
            shape((ROWS, features), BF),
        )
    else:
        out = shape((tokens, features), F32)
    return call(
        functools.partial(down_kernel, places, block, last, len(before)),
        out,
        [VMEM] * (2 + len(hiddens) + len(before)),
        weights,
        shared,
        *hiddens,
        *before,
        after=after,
    )


def fold_kernel(keep, far, *outs):
    for k, out in enumerate(outs):
        out[...] = (keep[k + 1] + far[k].astype(F32)).astype(out.dtype)


def finish_kernel(residual, keep, far, *rest):
    others, out = rest[:-1], rest[-1]
    half = lax.axis_index("grp") % 2
    value = residual[pl.ds(pl.multiple_of(half * ROWS, ROWS), ROWS), :] + keep[0] + far[...].astype(F32)
    for other in others:
        value = value + other[...].astype(F32)
    out[...] = value.astype(out.dtype)


def on_device(
    step_inputs,
    parents,
    routes,
    w_qkv,
    w_out,
    prompt_keys,
    prompt_values,
    prompt_parts,
    tail_keys,
    tail_values,
    w_router,
    norm_gain,
    w_gate_up,
    w_down,
):
    groups = lax.axis_size("grp")
    splits = lax.axis_size("exp")
    requests = groups // 2
    model = w_qkv.shape[0]
    width = w_qkv.shape[2]
    features = norm_gain.shape[0]
    local = w_gate_up.shape[0]
    tokens = requests * PAIR

    w_all = w_qkv.transpose(1, 0, 2)
    columns = call(
        columns_kernel,
        (
            shape((PAIR, PAIR), BF),
            shape((PREV * HALF, LANES), BF),
            shape((ROWS, LANES), BF),
        ),
        [],
        flops=HINT,
    )
    sent = call(
        send_kernel,
        shape((ROWS, model + LANES), BF),
        [VMEM] * 3,
        step_inputs[0],
        parents[0],
        routes[0],
        after=columns[:1],
    )
    came = exchanged(sent, "grp", 1)
    query, keys_new, values_new, part, tail_k, tail_v = call(
        own_kernel,
        (shape((ROWS, width), BF),) * 3
        + (shape((ROWS, features), F32),)
        + (shape((PREV * HALF, width), BF),) * 2,
        [VMEM] * 4,
        sent,
        w_all,
        tail_keys[0].transpose(1, 0, 2),
        tail_values[0].transpose(1, 0, 2),
        flops=HINT // 4,
    )
    near, x, named = call(
        attend_kernel,
        (
            shape((PAIR, width + LANES), BF),
            shape((PAIR, features), F32),
            shape((PAIR, LANES), F32),
        ),
        [SMEM] + [VMEM] * 14,
        prompt_parts,
        *columns,
        sent,
        came,
        query,
        part,
        w_all,
        keys_new,
        values_new,
        prompt_keys[0],
        prompt_values[0],
        tail_k,
        tail_v,
        flops=HINT,
    )
    far = exchanged(near, "grp", 1)
    remote = tuple(range(2, splits))
    close = (1, 0)
    joined, *terms = call(
        functools.partial(project_kernel, remote),
        (shape((PAIR, width), BF),) + tuple(shape((PAIR, features), BF) for _ in remote),
        [VMEM] * 3,
        near,
        far,
        w_out,
        flops=HINT,
    )
    beside, own_term = call(
        functools.partial(near_kernel, close),
        (shape((PAIR, features), BF), shape((PAIR, features), F32)),
        [VMEM] * 2,
        joined,
        w_out,
    )
    terms = [own_term, beside] + terms
    arrived = [exchanged(terms[k], "exp", k) for k in range(1, splits)]
    residual, message = call(
        residual_kernel,
        (shape((PAIR, features), F32), shape((PAIR, features + LANES), BF)),
        [VMEM] * (5 + len(arrived)),
        x,
        named,
        norm_gain.reshape(1, features),
        w_router.T,
        terms[0],
        *arrived,
        flops=HINT,
    )
    messages = [exchanged(message, "grp", 2 * k) for k in range(1, requests)]
    messages = [message] + messages
    picked, stats, target, choice = call(
        functools.partial(gather_kernel, local),
        (
            shape((local, EXPERTS * CAP_E // local, features), BF),
            shape((8, tokens), F32),
            shape((8, tokens), F32),
            shape((8, tokens), F32),
        ),
        [VMEM] * requests,
        *messages,
        scratch=[pltpu.VMEM((tokens, features), BF)],
        flops=HINT,
    )
    if splits == 4 and local == 2 * splits:
        gate = functools.partial(gate_block, weights=w_gate_up, picked=picked, block=2)
        (a0,) = gate(((3, 0),), stats=(stats,))
        far_a0 = exchanged(a0, "exp", 1)
        (a1,) = gate(((3, 1),), after=(a0,))
        far_a1 = exchanged(a1, "exp", 1)
        c0, stats = gate(((2, 0),), stats=(stats,), far=(far_a0,), after=(a1,))
        far_c0 = exchanged(c0, "exp", 2)
        (c1,) = gate(((2, 1),), far=(far_a1,), after=(c0,))
        far_c1 = exchanged(c1, "exp", 2)
        b0, d0 = gate(((1, 0), (0, 0)), dtypes=(BF, F32), after=(c1,), flops=30 * HINT // 100)
        far_b0 = exchanged(b0, "exp", 1)
        b1, d1 = gate(((1, 1), (0, 1)), dtypes=(BF, F32), after=(d0,), flops=30 * HINT // 100)
        far_b1 = exchanged(b1, "exp", 1)

        def hidden_of(pick, near, mid, far, after=()):
            return call(
                functools.partial(hidden_kernel, 2, pick),
                shape((near.shape[0], FFE), BF),
                [VMEM] * 6,
                near,
                mid,
                far,
                target,
                stats,
                far_c0,
                after=after,
                flops=10 * HINT // 100,
            )

        own0 = hidden_of(0, d0, far_b0, far_c0, after=(d1,))
        core0 = exchanged(own0, "exp", 1)
        y0 = exchanged(own0, "exp", 2)
        shared = call(
            functools.partial(place_kernel, local),
            shape((local, tokens, 2 * picked.shape[1]), BF),
            [VMEM] * 4,
            target,
            choice,
            stats,
            far_c0,
            after=(own0,),
            flops=10 * HINT // 100,
        )
        down = functools.partial(down_blocks, weights=w_down, shared=shared, block=2)
        own1 = hidden_of(1, d1, far_b1, far_c1, after=(shared,))
        core1 = exchanged(own1, "exp", 1)
        y1 = exchanged(own1, "exp", 2)
        mixed = down(((0, 0), (1, 0)), (own0, core0), after=(own1,))
        y0, mixed = lax.optimization_barrier((y0, mixed))
        far0 = exchanged(y0, "exp", 1)
        mixed = down(((0, 1), (1, 1), (2, 0)), (own1, core1, y0), before=(mixed,))
        y1, mixed = lax.optimization_barrier((y1, mixed))
        far1 = exchanged(y1, "exp", 1)
        mixed = down(((3, 0), (2, 1)), (far0, y1), before=(mixed,))
        keep, send, last_send = down(((3, 1),), (far1,), before=(mixed,), last=True)
    else:
        stats = lax.psum(stats, "exp")
        sums = jnp.einsum("lcd,ldf->lcf", picked, w_gate_up, preferred_element_type=F32)
        sums = lax.psum(sums.astype(BF), "exp").astype(F32)
        inverse = lax.rsqrt(stats[0] / model + EPSILON)
        goal, pick = target[:local], choice[:local]
        place = goal[:, None, :] == jnp.arange(picked.shape[1], dtype=F32)[None, :, None]
        sums = sums * jnp.sum(jnp.where(place, inverse, 0.0), axis=2, keepdims=True)
        hidden = (jax.nn.silu(sums[..., :FFE]) * sums[..., FFE:]).astype(BF)
        result = jnp.einsum("lcf,ldf->lcd", hidden, w_down, preferred_element_type=F32)
        share = jax.nn.softmax(stats[1:STATS] * inverse, axis=0)
        ids = jnp.arange(TOPK, dtype=F32)[None, :, None]
        weight = jnp.sum(jnp.where(pick[:, None, :] == ids, share[None], 0.0), axis=1)
        mixed = jnp.einsum(
            "lct,lcd->td",
            jnp.where(place, weight[:, None, :], 0.0),
            result.astype(BF).astype(F32),
            precision=lax.Precision.HIGHEST,
        )
        mixed = mixed.reshape(requests, 2, ROWS, features)
        half = lax.axis_index("grp") % 2
        keep = lax.dynamic_index_in_dim(mixed, half, 1, False)
        send = lax.dynamic_index_in_dim(mixed, 1 - half, 1, False).astype(BF)
        send, last_send = send[1:], send[0]
    folded = call(
        fold_kernel,
        tuple(shape((ROWS, features), BF) for _ in range(1, requests)),
        [VMEM] * 2,
        keep,
        exchanged(send, "grp", 1),
    )
    back = [exchanged(folded[k - 1], "grp", 2 * k) for k in range(1, requests)]
    result = call(
        finish_kernel,
        shape((ROWS, features), BF),
        [VMEM] * (3 + len(back)),
        residual,
        keep,
        exchanged(last_send, "grp", 1),
        *back[::-1],
    )
    return result.reshape(1, STEPS, HALF, features)


def solution(mesh):
    placed = (
        P("grp", None, None, None),
        P("grp", None, None),
        P("grp", None, None, None),
        P(None, None, "exp"),
        P("exp", None),
        P("grp", None, "exp"),
        P("grp", None, "exp"),
        P("grp"),
        P("grp", None, None, "exp"),
        P("grp", None, None, "exp"),
        P("exp", None),
        P("exp"),
        P("grp", "exp", None),
        P("grp", "exp", None),
    )
    return jax.shard_map(
        on_device,
        mesh=mesh,
        in_specs=placed,
        out_specs=P("grp", None, None, "exp"),
        check_vma=False,
    )
```
